256 devices in a mesh: seq: 128 (over y_lo, x, z, core), dp: 2 (over y_hi).
Axes of the slice: x: 4, y: 4 (y_hi: 2, y_lo: 2; y = y_hi * 2 + y_lo), z: 8, core: 2. Of those that a mesh axis runs over, the one named last changes fastest.
Arguments:
- inputs: bfloat16 [2, 65536, 512], P('dp', 'seq'), may hold values from -6 to 6
- filter_taps: float32 [6, 2, 512], replicated, may hold values from -3 to 3
- mixing: bfloat16 [6, 512, 512], replicated, may hold values from -0.25 to 0.25
- cotangent: bfloat16 [2, 65536, 512], P('dp', 'seq'), may hold values from -6 to 6
Outputs:
- grad_inputs: float32 [2, 65536, 512], P('dp', 'seq')
- grad_taps: float32 [6, 2, 512], replicated
- grad_mixing: bfloat16 [6, 512, 512], replicated
The draws below stay inside these ranges and needn't reach their ends.
All inputs are finite; a program needn't handle non-finite values.
Results may differ from the reference program's by a relative error of at most 0.014.
Values may be sent and summed in bfloat16 or wider, within the bound.
A program may use at most 64 MiB of HBM per device.

```python
import jax
import jax.numpy as jnp
from jax import lax

C = 512
TOK_DEV = 512
LEVELS = 6
SEQLEN = 65536
BATCH = 2


def block_scale(rng, extent, shards, low, largest):
    def one(dim, blocks):
        steps = jax.random.uniform(jax.random.fold_in(jax.random.fold_in(rng, 6), dim), (blocks,), jnp.float32, low / len(shards), largest / len(shards))
        return jnp.repeat(jnp.exp(steps), extent[dim] // blocks).reshape((-1,) + (1,) * (len(extent) - dim - 1))

    loudness = one(*shards[0])
    for cut in shards[1:]:
        loudness = loudness * one(*cut)
    return loudness


def gaussian(rng, extent, width, limit, shards=(), held_as=jnp.bfloat16):
    entries = width * jax.random.normal(rng, extent, jnp.float32)
    if shards:
        entries = entries * block_scale(rng, extent, shards, -0.22, 0.18)
    return jnp.clip(entries, -limit, limit).astype(held_as)


def setup_inputs(seed: int = 0) -> dict:
    seeds = jax.random.split(jax.random.key(seed), 5)
    inputs = gaussian(seeds[0], (BATCH, SEQLEN, C), 1.0, 6.0, ((0, 2), (1, 128)))
    filter_taps = gaussian(seeds[1], (LEVELS, 2, C), 0.7, 3.0, (), jnp.float32)
    mixing = gaussian(seeds[2], (LEVELS, C, C), C ** -0.5, 0.25)
    cotangent = gaussian(seeds[3], (BATCH, SEQLEN, C), 1.0, 6.0, ((0, 2), (1, 128)))
    return dict(inputs=inputs, filter_taps=filter_taps, mixing=mixing, cotangent=cotangent)


def shift_back(values, distance):
    padded = jnp.pad(values, ((0, 0), (distance, 0), (0, 0)))
    return padded[:, :values.shape[1], :]

def shift_ahead(values, distance):
    padded = jnp.pad(values, ((0, 0), (0, distance), (0, 0)))
    return padded[:, distance:, :]

def gelu_tanh(values):
    return jax.nn.gelu(values, approximate=True)

def reference(inputs, filter_taps, mixing, cotangent):
    batch, length, channels = inputs.shape
    levels = mixing.shape[0]
    current = inputs
    stored = []
    for layer_idx in range(levels):
        distance = TOK_DEV * 2 ** layer_idx // 4
        stored.append(current)
        lagged = shift_back(current, distance)
        preact = filter_taps[layer_idx, 0] * current.astype(jnp.float32) + filter_taps[layer_idx, 1] * lagged.astype(jnp.float32)
        act = gelu_tanh(preact).astype(jnp.bfloat16)
        mixed = jnp.dot(act.reshape(-1, channels), mixing[layer_idx], preferred_element_type=jnp.float32)
        current = (current.astype(jnp.float32) + mixed.reshape(batch, length, channels)).astype(jnp.bfloat16)
    grad_out = cotangent.astype(jnp.float32)
    tap_list = []
    mix_list = []
    for layer_idx in reversed(range(levels)):
        distance = TOK_DEV * 2 ** layer_idx // 4
        current = stored[layer_idx]
        lagged = shift_back(current, distance)
        preact = filter_taps[layer_idx, 0] * current.astype(jnp.float32) + filter_taps[layer_idx, 1] * lagged.astype(jnp.float32)
        act = gelu_tanh(preact).astype(jnp.bfloat16)
        grad_bf = grad_out.astype(jnp.bfloat16).reshape(-1, channels)
        mix_list.append(jnp.dot(act.reshape(-1, channels).T, grad_bf, preferred_element_type=jnp.float32))
        grad_act = jnp.dot(grad_bf, mixing[layer_idx].T, preferred_element_type=jnp.float32).reshape(batch, length, channels)
        grad_pre = jax.vjp(gelu_tanh, preact)[1](grad_act)[0]
        tap_now = lax.optimization_barrier(jnp.sum(grad_pre * current.astype(jnp.float32), axis=(0, 1)))
        tap_lag = lax.optimization_barrier(jnp.sum(grad_pre * lagged.astype(jnp.float32), axis=(0, 1)))
        tap_list.append(jnp.stack([tap_now, tap_lag]))
        lag_grad = (filter_taps[layer_idx, 1] * grad_pre).astype(jnp.bfloat16)
        grad_out = grad_out + filter_taps[layer_idx, 0] * grad_pre + shift_ahead(lag_grad, distance).astype(jnp.float32)
    grad_taps = jnp.stack(tap_list[::-1])
    grad_mixing = jnp.stack(mix_list[::-1]).astype(jnp.bfloat16)
    return (grad_out, grad_taps, grad_mixing)
```

```python
import functools, jax, jax.numpy as jnp
from jax import lax
from jax.experimental import pallas as pl
from jax.experimental.pallas import tpu as pltpu
MESH = pl.DeviceIdType.MESH
CHIPS = 64

def coords():
    me = lax.axis_index("seq")
    c = lax.rem(me, 2)
    z = lax.rem(lax.div(me, 2), 8)
    x = lax.rem(lax.div(me, 16), 4)
    w = lax.div(me, 64)
    h = lax.axis_index("dp")
    return h, w, x, z, c

def place(h, w, x, z, c):
    return {"seq": ((w * 4 + x) * 8 + z) * 2 + c, "dp": h}

def signal(sem, dev):
    pl.semaphore_signal(sem, inc=1, device_id=dev, device_id_type=MESH)

def enter(plane_sem, all_sem):
    h, w, x, z, c = coords()
    bar = pltpu.get_barrier_semaphore()
    signal(bar, place(h, w, x, z, 1 - c))
    @pl.loop(1, 8)
    def _(k):
        signal(bar, place(h, w, x, lax.rem(z + k, 8), c))
    @pl.loop(1, 4)
    def _(k):
        signal(bar, place(h, w, lax.rem(x + k, 4), z, c))
    signal(bar, place(h, 1 - w, x, z, c))
    pl.semaphore_wait(bar, 12)
    @pl.loop(1, 4)
    def _(k):
        signal(plane_sem, place(h, w, lax.rem(x + k, 4), z, c))
    pl.semaphore_wait(plane_sem, 3)
    signal(all_sem, place(h, 1 - w, x, z, c))
    pl.semaphore_wait(all_sem, 1)

def selection(out_of, shape=(256, 256)):
    o = lax.broadcasted_iota(jnp.int32, shape, 0)
    i = lax.broadcasted_iota(jnp.int32, shape, 1)
    return jnp.where(i == out_of(o), 1.0, 0.0).astype(jnp.bfloat16)

def tokens_to_tiles(a_ref, mine, other, c):
    def src(o):
        half, j, cg, n = o // 128, (o // 16) % 8, (o // 4) % 4, o % 4
        return (n * 4 + cg) * 16 + 2 * j + jnp.where(half == 0, c, 1 - c)
    pm = selection(src)
    @pl.loop(0, 8)
    def _(g):
        m = jnp.concatenate([a_ref[pl.ds(pl.multiple_of(n * 128 + g * 16, 16), 16), cg * 128:(cg + 1) * 128] for n in range(4) for cg in range(4)], axis=0)
        t = jnp.dot(pm, m, preferred_element_type=jnp.float32).astype(jnp.bfloat16).reshape(2, 8, 16, 128)
        mine[pl.ds(g * 8, 8), c] = t[0]
        other[pl.ds(g * 8, 8)] = t[1]

def tiles_to_rows(r_ref, put):
    qm = selection(lambda o: ((o // 4) % 16 * 4 + o // 64) * 4 + o % 4)
    @pl.loop(0, 8)
    def _(g):
        m = r_ref[pl.ds(g * 8, 8)].reshape(256, 128)
        t = jnp.dot(qm, m, preferred_element_type=jnp.float32)
        for cg in range(4):
            put(g, cg, t[cg * 64:(cg + 1) * 64])

def rows_to_tiles(g_ref, mine, other, c):
    def src(o):
        half, j, cg, n = o // 128, (o // 16) % 8, (o // 4) % 4, o % 4
        return (cg * 16 + 2 * j + jnp.where(half == 0, c, 1 - c)) * 4 + n
    pm = selection(src)
    @pl.loop(0, 8)
    def _(g):
        m = jnp.concatenate([g_ref[pl.ds(pl.multiple_of(g * 64, 64), 64), cg * 128:(cg + 1) * 128] for cg in range(4)], axis=0)
        t = jnp.dot(pm, m, preferred_element_type=jnp.float32).astype(jnp.bfloat16).reshape(2, 8, 16, 128)
        mine[pl.ds(g * 8, 8), c] = t[0]
        other[pl.ds(g * 8, 8)] = t[1]

def tiles_to_tokens(r_ref, o_ref):
    qm = selection(lambda o: (o % 16 * 4 + (o // 16) % 4) * 4 + o // 64)
    @pl.loop(0, 8)
    def _(g):
        m = r_ref[pl.ds(g * 8, 8)].reshape(256, 128)
        t = jnp.dot(qm, m, preferred_element_type=jnp.float32)
        for n in range(4):
            for cg in range(4):
                o_ref[pl.ds(pl.multiple_of(n * 128 + g * 16, 16), 16), cg * 128:(cg + 1) * 128] = t[(n * 4 + cg) * 16:(n * 4 + cg + 1) * 16]

def pair_copy(other, s_ref, sems, k):
    h, w, x, z, c = coords()
    return pltpu.make_async_remote_copy(other, s_ref.at[:, c], sems.at[0, k], sems.at[1, k], device_id=place(h, w, x, z, 1 - c), device_id_type=MESH)

def spread(s_ref, r_ref, sems, loc, k):
    h, w, x, z, c = coords()
    j = (w * 4 + x) * 8 + z
    pltpu.make_async_copy(s_ref.at[j], r_ref.at[j], loc.at[k]).start()
    @pl.loop(1, 64)
    def _(t):
        b = lax.rem(t, 8)
        a = lax.div(t, 8)
        dz = jnp.where(lax.rem(b, 2) == 1, lax.div(b + 1, 2), 8 - lax.div(b, 2))
        z2 = lax.rem(z + dz, 8)
        x2 = lax.rem(x + lax.rem(a, 4), 4)
        w2 = lax.rem(w + lax.div(a, 4), 2)
        pltpu.make_async_remote_copy(s_ref.at[(w2 * 4 + x2) * 8 + z2], r_ref.at[j], sems.at[0, k], sems.at[1, k], device_id=place(h, w2, x2, z2, c), device_id_type=MESH).start()

def spread_arrived(s_ref, r_ref, sems, loc, k):
    h, w, x, z, c = coords()
    j = (w * 4 + x) * 8 + z
    pltpu.make_async_copy(s_ref.at[j], r_ref.at[j], loc.at[k]).wait()
    pltpu.make_async_copy(s_ref.at[pl.ds(0, 63)], r_ref.at[pl.ds(0, 63)], sems.at[1, k]).wait()

def spread_sent(s_ref, r_ref, sems, k):
    pltpu.make_async_copy(s_ref.at[pl.ds(0, 63)], r_ref.at[pl.ds(0, 63)], sems.at[0, k]).wait()

def k1(x_ref, g_ref, xo_ref, go_ref, ox, sx, rx, og, sg, rg, pair_sems, sems, loc, plane_sem, all_sem):
    h, w, x, z, c = coords()
    tokens_to_tiles(x_ref, sx, ox, c)
    enter(plane_sem, all_sem)
    px = pair_copy(ox, sx, pair_sems, 0)
    px.start()
    tokens_to_tiles(g_ref, sg, og, c)
    pg = pair_copy(og, sg, pair_sems, 1)
    pg.start()
    px.wait_recv()
    spread(sx, rx, sems, loc, 0)
    pg.wait_recv()
    spread(sg, rg, sems, loc, 1)
    spread_arrived(sx, rx, sems, loc, 0)
    def put(o_ref):
        def f(g, cg, t):
            o_ref[pl.ds(pl.multiple_of(g * 64, 64), 64), cg * 128:(cg + 1) * 128] = t.astype(jnp.bfloat16)
        return f
    tiles_to_rows(rx, put(xo_ref))
    spread_arrived(sg, rg, sems, loc, 1)
    tiles_to_rows(rg, put(go_ref))
    px.wait_send(); pg.wait_send()
    spread_sent(sx, rx, sems, 0)
    spread_sent(sg, rg, sems, 1)

VM = pl.BlockSpec(memory_space=pltpu.VMEM)
def relayout(xs, gs, cid=1):
    bf = jnp.bfloat16
    b = lambda *s: pltpu.VMEM(s, bf)
    return pl.pallas_call(k1, out_shape=[jax.ShapeDtypeStruct((512, 512), bf)] * 2, in_specs=[VM] * 2, out_specs=[VM] * 2,
        scratch_shapes=[b(64, 16, 128), b(64, 2, 16, 128), b(64, 2, 16, 128)] * 2 + [pltpu.SemaphoreType.DMA((2, 2)), pltpu.SemaphoreType.DMA((2, 2)), pltpu.SemaphoreType.DMA((2,)), pltpu.SemaphoreType.REGULAR, pltpu.SemaphoreType.REGULAR],
        compiler_params=pltpu.CompilerParams(collective_id=cid, has_side_effects=True, vmem_limit_bytes=40 << 20))(xs, gs)

def k3(g_ref, o_ref, og, sg, rg, pair_sems, sems, loc, plane_sem, all_sem):
    h, w, x, z, c = coords()
    rows_to_tiles(g_ref, sg, og, c)
    enter(plane_sem, all_sem)
    pg = pair_copy(og, sg, pair_sems, 0)
    pg.start()
    pg.wait_recv()
    spread(sg, rg, sems, loc, 0)
    spread_arrived(sg, rg, sems, loc, 0)
    tiles_to_tokens(rg, o_ref)
    pg.wait_send()
    spread_sent(sg, rg, sems, 0)

def back(gs, cid=2):
    bf = jnp.bfloat16
    b = lambda *s: pltpu.VMEM(s, bf)
    return pl.pallas_call(k3, out_shape=jax.ShapeDtypeStruct((512, 512), jnp.float32), in_specs=[VM], out_specs=VM,
        scratch_shapes=[b(64, 16, 128), b(64, 2, 16, 128), b(64, 2, 16, 128)] + [pltpu.SemaphoreType.DMA((2, 1)), pltpu.SemaphoreType.DMA((2, 1)), pltpu.SemaphoreType.DMA((1,)), pltpu.SemaphoreType.REGULAR, pltpu.SemaphoreType.REGULAR],
        compiler_params=pltpu.CompilerParams(collective_id=cid, has_side_effects=True, vmem_limit_bytes=40 << 20))(gs)

def gelu_tanh(values):
    return jax.nn.gelu(values, approximate=True)

def delayed(v, d):
    return jnp.concatenate([jnp.zeros((d, v.shape[1]), v.dtype), v[:-d]], axis=0)

def hastened(v, d):
    return jnp.concatenate([v[d:], jnp.zeros((d, v.shape[1]), v.dtype)], axis=0)

def local(inputs, filter_taps, mixing, cotangent):
    f32, bf = jnp.float32, jnp.bfloat16
    current, cot = relayout(inputs[0], cotangent[0])
    stored = []
    for l in range(6):
        lagged = delayed(current, 1 << l)
        stored.append((current, lagged))
        pre = filter_taps[l, 0] * current.astype(f32) + filter_taps[l, 1] * lagged.astype(f32)
        act = gelu_tanh(pre).astype(bf)
        current = (current.astype(f32) + jnp.dot(act, mixing[l], preferred_element_type=f32)).astype(bf)
    g = cot.astype(f32)
    taps, mixes = [], []
    for l in reversed(range(6)):
        current, lagged = stored[l]
        pre = filter_taps[l, 0] * current.astype(f32) + filter_taps[l, 1] * lagged.astype(f32)
        act = gelu_tanh(pre).astype(bf)
        gb = g.astype(bf)
        mixes.append(lax.dot_general(act, gb, (((0,), (0,)), ((), ())), preferred_element_type=f32))
        gact = jnp.dot(gb, mixing[l].T, preferred_element_type=f32)
        gpre = jax.vjp(gelu_tanh, pre)[1](gact)[0]
        taps.append(jnp.stack([jnp.sum(gpre * current.astype(f32), axis=0), jnp.sum(gpre * lagged.astype(f32), axis=0)]))
        lag = (filter_taps[l, 1] * gpre).astype(bf)
        g = g + filter_taps[l, 0] * gpre + hastened(lag, 1 << l).astype(f32)
    grad_inputs = back(g.astype(bf))[None]
    gt, gm = lax.psum((jnp.stack(taps[::-1]), jnp.stack(mixes[::-1])), ("seq", "dp"))
    return grad_inputs, gt, gm.astype(bf)

def solution(mesh):
    from jax.sharding import PartitionSpec as P
    return jax.shard_map(local, mesh=mesh, in_specs=(P("dp", "seq", None), P(), P(), P("dp", "seq", None)),
        out_specs=(P("dp", "seq", None), P(), P()), check_vma=False)
```

```python
import functools, jax, jax.numpy as jnp
from jax import lax
from jax.sharding import PartitionSpec as P
from jax.experimental import pallas as pl
from jax.experimental.pallas import tpu as pltpu
MESH = pl.DeviceIdType.MESH
CHIPS = 64

def coords():
    me = lax.axis_index("seq")
    c = lax.rem(me, 2)
    z = lax.rem(lax.div(me, 2), 8)
    x = lax.rem(lax.div(me, 16), 4)
    w = lax.div(me, 64)
    h = lax.axis_index("dp")
    return h, w, x, z, c

def place(h, w, x, z, c):
    return {"seq": ((w * 4 + x) * 8 + z) * 2 + c, "dp": h}

def on_y(y, x, z, c):
    return place(lax.div(y, 2), lax.rem(y, 2), x, z, c)

def signal(sem, dev):
    pl.semaphore_signal(sem, inc=1, device_id=dev, device_id_type=MESH)

def enter(plane_sem, all_sem):
    h, w, x, z, c = coords()
    bar = pltpu.get_barrier_semaphore()
    signal(bar, place(h, w, x, z, 1 - c))
    @pl.loop(1, 8)
    def _(k):
        signal(bar, place(h, w, x, lax.rem(z + k, 8), c))
    @pl.loop(1, 4)
    def _(k):
        signal(bar, place(h, w, lax.rem(x + k, 4), z, c))
    y = h * 2 + w
    @pl.loop(1, 4)
    def _(k):
        signal(bar, on_y(lax.rem(y + k, 4), x, z, c))
    pl.semaphore_wait(bar, 14)
    @pl.loop(1, 4)
    def _(k):
        signal(plane_sem, place(h, w, lax.rem(x + k, 4), z, c))
    pl.semaphore_wait(plane_sem, 3)
    signal(all_sem, place(h, 1 - w, x, z, c))
    pl.semaphore_wait(all_sem, 1)

def selection(out_of, shape=(256, 256)):
    o = lax.broadcasted_iota(jnp.int32, shape, 0)
    i = lax.broadcasted_iota(jnp.int32, shape, 1)
    return jnp.where(i == out_of(o), 1.0, 0.0).astype(jnp.bfloat16)

def tokens_to_tiles(a_ref, mine, other, c):
    def src(o):
        half, j, cg, n = o // 128, (o // 16) % 8, (o // 4) % 4, o % 4
        return (n * 4 + cg) * 16 + 2 * j + jnp.where(half == 0, c, 1 - c)
    pm = selection(src)
    @pl.loop(0, 8)
    def _(g):
        m = jnp.concatenate([a_ref[pl.ds(pl.multiple_of(n * 128 + g * 16, 16), 16), cg * 128:(cg + 1) * 128] for n in range(4) for cg in range(4)], axis=0)
        t = jnp.dot(pm, m, preferred_element_type=jnp.float32).astype(jnp.bfloat16).reshape(2, 8, 16, 128)
        mine[pl.ds(g * 8, 8), c] = t[0]
        other[pl.ds(g * 8, 8)] = t[1]

def tiles_to_rows(r_ref, put):
    qm = selection(lambda o: ((o // 4) % 16 * 4 + o // 64) * 4 + o % 4)
    @pl.loop(0, 8)
    def _(g):
        m = r_ref[pl.ds(g * 8, 8)].reshape(256, 128)
        t = jnp.dot(qm, m, preferred_element_type=jnp.float32)
        for cg in range(4):
            put(g, cg, t[cg * 64:(cg + 1) * 64])

def rows_to_tiles(g_ref, mine, other, c):
    def src(o):
        half, j, cg, n = o // 128, (o // 16) % 8, (o // 4) % 4, o % 4
        return (cg * 16 + 2 * j + jnp.where(half == 0, c, 1 - c)) * 4 + n
    pm = selection(src)
    @pl.loop(0, 8)
    def _(g):
        m = jnp.concatenate([g_ref[pl.ds(pl.multiple_of(g * 64, 64), 64), cg * 128:(cg + 1) * 128] for cg in range(4)], axis=0)
        t = jnp.dot(pm, m, preferred_element_type=jnp.float32).astype(jnp.bfloat16).reshape(2, 8, 16, 128)
        mine[pl.ds(g * 8, 8), c] = t[0]
        other[pl.ds(g * 8, 8)] = t[1]

def tiles_to_tokens(r_ref, o_ref):
    qm = selection(lambda o: (o % 16 * 4 + (o // 16) % 4) * 4 + o // 64)
    @pl.loop(0, 8)
    def _(g):
        m = r_ref[pl.ds(g * 8, 8)].reshape(256, 128)
        t = jnp.dot(qm, m, preferred_element_type=jnp.float32)
        for n in range(4):
            for cg in range(4):
                o_ref[pl.ds(pl.multiple_of(n * 128 + g * 16, 16), 16), cg * 128:(cg + 1) * 128] = t[(n * 4 + cg) * 16:(n * 4 + cg + 1) * 16]

def pair_copy(other, s_ref, sems, k):
    h, w, x, z, c = coords()
    return pltpu.make_async_remote_copy(other, s_ref.at[:, c], sems.at[0, k], sems.at[1, k], device_id=place(h, w, x, z, 1 - c), device_id_type=MESH)

def spread(s_ref, r_ref, sems, loc, k, begin=1, end=64):
    h, w, x, z, c = coords()
    j = (w * 4 + x) * 8 + z
    if begin == 1:
        pltpu.make_async_copy(s_ref.at[j], r_ref.at[j], loc.at[k]).start()
    @pl.loop(begin, end)
    def _(t):
        b = lax.rem(t, 8)
        a = lax.div(t, 8)
        dz = jnp.where(lax.rem(b, 2) == 1, lax.div(b + 1, 2), 8 - lax.div(b, 2))
        z2 = lax.rem(z + dz, 8)
        x2 = lax.rem(x + lax.rem(a, 4), 4)
        w2 = lax.rem(w + lax.div(a, 4), 2)
        pltpu.make_async_remote_copy(s_ref.at[(w2 * 4 + x2) * 8 + z2], r_ref.at[j], sems.at[0, k], sems.at[1, k], device_id=place(h, w2, x2, z2, c), device_id_type=MESH).start()

def spread_arrived(s_ref, r_ref, sems, loc, k):
    h, w, x, z, c = coords()
    j = (w * 4 + x) * 8 + z
    pltpu.make_async_copy(s_ref.at[j], r_ref.at[j], loc.at[k]).wait()
    pltpu.make_async_copy(s_ref.at[pl.ds(0, 63)], r_ref.at[pl.ds(0, 63)], sems.at[1, k]).wait()

def spread_sent(s_ref, r_ref, sems, k):
    pltpu.make_async_copy(s_ref.at[pl.ds(0, 63)], r_ref.at[pl.ds(0, 63)], sems.at[0, k]).wait()

LEVELS = 6
K0 = 0.7978845608028654
K1C = K0 * 0.044715
PAD = 32
TILE = 128

def forward(l, xf, act, dg, taps_ref, mix_ref):
    d = 1 << l
    for rt in range(512 // TILE):
        r0 = rt * TILE
        for cg in range(4):
            lanes = slice(cg * 128, cg * 128 + 128)
            cur = xf[l, cg, PAD + r0:PAD + r0 + TILE]
            lag = xf[l, cg, PAD + r0 - d:PAD + r0 - d + TILE]
            p = taps_ref[l, 0:1, lanes] * cur + taps_ref[l, 1:2, lanes] * lag
            p2 = p * p
            t = jnp.tanh(p * (K0 + K1C * p2))
            half = 0.5 + 0.5 * t
            act[l, r0:r0 + TILE, lanes] = (p * half).astype(jnp.bfloat16)
            dg[l, cg, r0:r0 + TILE] = half + (half * (1.0 - half) * p) * (2 * K0 + 6 * K1C * p2)
        if l + 1 < LEVELS:
            m = jnp.dot(act[l, r0:r0 + TILE, :], mix_ref[l], preferred_element_type=jnp.float32)
            for cg in range(4):
                nxt = xf[l, cg, PAD + r0:PAD + r0 + TILE] + m[:, cg * 128:cg * 128 + 128]
                xf[l + 1, cg, PAD + r0:PAD + r0 + TILE] = nxt.astype(jnp.bfloat16).astype(jnp.float32)

def backward(l, xf, dg, g, gb, lag, taps_ref, mix_ref, gtaps):
    d = 1 << l
    sums = [[jnp.zeros((8, 128), jnp.float32) for _ in range(2)] for _ in range(4)]
    for rt in reversed(range(512 // TILE)):
        r0 = rt * TILE
        ga = lax.dot_general(gb[r0:r0 + TILE, :], mix_ref[l], (((1,), (1,)), ((), ())), preferred_element_type=jnp.float32)
        for cg in range(4):
            lanes = slice(cg * 128, cg * 128 + 128)
            gp = ga[:, lanes] * dg[l, cg, r0:r0 + TILE]
            cur = xf[l, cg, PAD + r0:PAD + r0 + TILE]
            old = xf[l, cg, PAD + r0 - d:PAD + r0 - d + TILE]
            sums[cg][0] += jnp.sum((gp * cur).reshape(TILE // 8, 8, 128), axis=0)
            sums[cg][1] += jnp.sum((gp * old).reshape(TILE // 8, 8, 128), axis=0)
            lag[cg, r0:r0 + TILE] = (taps_ref[l, 1:2, lanes] * gp).astype(jnp.bfloat16).astype(jnp.float32)
            new = g[cg, r0:r0 + TILE] + taps_ref[l, 0:1, lanes] * gp + lag[cg, r0 + d:r0 + d + TILE]
            g[cg, r0:r0 + TILE] = new
            gb[r0:r0 + TILE, lanes] = new.astype(jnp.bfloat16)
    for cg in range(4):
        for k in range(2):
            gtaps[2 * l + k:2 * l + k + 1, cg * 128:cg * 128 + 128] = jnp.sum(sums[cg][k], axis=0, keepdims=True)

def mix_grad(l, act, gb):
    return lax.dot_general(act[l], gb[...], (((0,), (0,)), ((), ())), preferred_element_type=jnp.float32)


VM = pl.BlockSpec(memory_space=pltpu.VMEM)

class Reduction:
    def __init__(self, gm, out, c0, hh, r1, qq, r2, e8, r3, f8, ss, rs):
        self.__dict__.update(gm=gm, out=out, c0=c0, hh=hh, r1=r1, qq=qq, r2=r2, e8=e8, r3=r3, f8=f8, ss=ss, rs=rs)
        self.h, self.w, self.x, self.z, self.c = coords()
        self.y = self.h * 2 + self.w

    def first(self, l):
        return self.x if l % 2 else self.y

    def second(self, l):
        return self.y if l % 2 else self.x

    def on(self, along_x, i):
        if along_x:
            return place(self.h, self.w, i, self.z, self.c)
        return on_y(i, self.x, self.z, self.c)

    def copy(self, src, dst, l, stage, dev):
        return pltpu.make_async_remote_copy(src, dst, self.ss.at[l, stage], self.rs.at[l, stage], device_id=dev, device_id_type=MESH)

    def other_core(self):
        return place(self.h, self.w, self.x, self.z, 1 - self.c)

    def rows(self, l):
        r256 = self.c * 256
        r64 = r256 + self.first(l) * 64
        return pl.multiple_of(r256, 256), pl.multiple_of(r64, 64), pl.multiple_of(r64 + self.second(l) * 16, 16)

    def took(self, ref, l, stage):
        pltpu.make_async_copy(ref, ref, self.rs.at[l, stage]).wait()

    def gave(self, ref, l, stage):
        pltpu.make_async_copy(ref, ref, self.ss.at[l, stage]).wait()

    def halve(self, l):
        far = pl.multiple_of((1 - self.c) * 256, 256)
        self.copy(self.gm.at[l, pl.ds(far, 256)], self.c0.at[l], l, 0, self.other_core()).start()

    def quarter(self, l):
        self.took(self.c0.at[l], l, 0)
        near = self.rows(l)[0]
        self.hh[l] = (self.gm[l, pl.ds(near, 256)].astype(jnp.float32) + self.c0[l].astype(jnp.float32)).astype(jnp.bfloat16)
        i = self.first(l)
        @pl.loop(1, 4)
        def _(k):
            j = lax.rem(i + k, 4)
            self.copy(self.hh.at[l, pl.ds(pl.multiple_of(j * 64, 64), 64)], self.r1.at[l, i], l, 1, self.on(l % 2, j)).start()

    def sixteenth(self, l):
        self.took(self.r1.at[l, pl.ds(0, 3)], l, 1)
        i = self.first(l)
        s = self.hh[l, pl.ds(pl.multiple_of(i * 64, 64), 64)].astype(jnp.float32)
        for k in range(1, 4):
            s += self.r1[l, lax.rem(i + k, 4)].astype(jnp.float32)
        self.qq[l] = s.astype(jnp.bfloat16)
        i2 = self.second(l)
        @pl.loop(1, 4)
        def _(k):
            j = lax.rem(i2 + k, 4)
            self.copy(self.qq.at[l, pl.ds(pl.multiple_of(j * 16, 16), 16)], self.r2.at[l, i2], l, 2, self.on(1 - l % 2, j)).start()

    def tile(self, p):
        z = self.z
        for l in (2 * p, 2 * p + 1):
            self.took(self.r2.at[l, pl.ds(0, 3)], l, 2)
            i2 = self.second(l)
            s = self.qq[l, pl.ds(pl.multiple_of(i2 * 16, 16), 16)].astype(jnp.float32)
            for k in range(1, 4):
                s += self.r2[l, lax.rem(i2 + k, 4)].astype(jnp.float32)
            for cg in range(4):
                self.e8[p, l % 2 * 4 + cg] = s[:, cg * 128:cg * 128 + 128].astype(jnp.bfloat16)
        @pl.loop(1, 8)
        def _(k):
            j = lax.rem(z + k, 8)
            self.copy(self.e8.at[p, j], self.r3.at[p, z], 2 * p, 3, place(self.h, self.w, self.x, j, self.c)).start()

    def untile(self, p):
        z = self.z
        self.took(self.r3.at[p, pl.ds(0, 7)], 2 * p, 3)
        s = self.e8[p, z].astype(jnp.float32)
        for k in range(1, 8):
            s += self.r3[p, lax.rem(z + k, 8)].astype(jnp.float32)
        self.f8[p, z] = s.astype(jnp.bfloat16)
        @pl.loop(1, 8)
        def _(k):
            j = lax.rem(z + k, 8)
            self.copy(self.f8.at[p, z], self.f8.at[p, z], 2 * p, 4, place(self.h, self.w, self.x, j, self.c)).start()

    def unsixteenth(self, p):
        self.took(self.f8.at[p, pl.ds(0, 7)], 2 * p, 4)
        for l in (2 * p, 2 * p + 1):
            r16 = self.rows(l)[2]
            for cg in range(4):
                self.out[l, pl.ds(r16, 16), cg * 128:cg * 128 + 128] = self.f8[p, l % 2 * 4 + cg]
            mine = self.out.at[l, pl.ds(r16, 16)]
            i2 = self.second(l)
            @pl.loop(1, 4)
            def _(k):
                self.copy(mine, mine, l, 5, self.on(1 - l % 2, lax.rem(i2 + k, 4))).start()

    def unquarter(self, p):
        for l in (2 * p, 2 * p + 1):
            self.took(self.out.at[l, pl.ds(0, 48)], l, 5)
            mine = self.out.at[l, pl.ds(self.rows(l)[1], 64)]
            i = self.first(l)
            @pl.loop(1, 4)
            def _(k):
                self.copy(mine, mine, l, 6, self.on(l % 2, lax.rem(i + k, 4))).start()

    def unhalve(self, p):
        for l in (2 * p, 2 * p + 1):
            self.took(self.out.at[l, pl.ds(0, 192)], l, 6)
            mine = self.out.at[l, pl.ds(self.rows(l)[0], 256)]
            self.copy(mine, mine, l, 7, self.other_core()).start()

    def finish(self, p):
        for l in (2 * p, 2 * p + 1):
            self.took(self.out.at[l, pl.ds(0, 256)], l, 7)
            self.gave(self.c0.at[l], l, 0)
            self.gave(self.r1.at[l, pl.ds(0, 3)], l, 1)
            self.gave(self.r2.at[l, pl.ds(0, 3)], l, 2)
            self.gave(self.out.at[l, pl.ds(0, 48)], l, 5)
            self.gave(self.out.at[l, pl.ds(0, 192)], l, 6)
            self.gave(self.out.at[l, pl.ds(0, 256)], l, 7)
        self.gave(self.r3.at[p, pl.ds(0, 7)], 2 * p, 3)
        self.gave(self.f8.at[p, pl.ds(0, 7)], 2 * p, 4)

class TapSums:
    def __init__(self, bufs, ss, rs):
        self.bufs, self.ss, self.rs = bufs, ss, rs
        self.h, self.w, self.x, self.z, self.c = coords()
        self.at = (self.c, self.x, self.h * 2 + self.w, self.z)
        self.size = (2, 4, 4, 8)

    def dev(self, stage, j):
        if stage == 0:
            return place(self.h, self.w, self.x, self.z, j)
        if stage == 1:
            return place(self.h, self.w, j, self.z, self.c)
        if stage == 2:
            return on_y(j, self.x, self.z, self.c)
        return place(self.h, self.w, self.x, j, self.c)

    def send(self, stage, value):
        n, i, buf = self.size[stage], self.at[stage], self.bufs[stage]
        buf[i] = value
        @pl.loop(1, n)
        def _(k):
            pltpu.make_async_remote_copy(buf.at[i], buf.at[i], self.ss.at[stage], self.rs.at[stage],
                device_id=self.dev(stage, lax.rem(i + k, n)), device_id_type=MESH).start()

    def total(self, stage):
        n, buf = self.size[stage], self.bufs[stage]
        part = buf.at[pl.ds(0, n - 1)]
        pltpu.make_async_copy(part, part, self.rs.at[stage]).wait()
        s = buf[0]
        for k in range(1, n):
            s += buf[k]
        return s

    def finish(self):
        for stage in range(4):
            part = self.bufs[stage].at[pl.ds(0, self.size[stage] - 1)]
            pltpu.make_async_copy(part, part, self.ss.at[stage]).wait()

def reduction_scratch():
    b = lambda *s: pltpu.VMEM(s, jnp.bfloat16)
    D = pltpu.SemaphoreType.DMA
    return [b(6, 512, 512), b(6, 256, 512), b(6, 256, 512), b(6, 4, 64, 512), b(6, 64, 512), b(6, 4, 16, 512), b(3, 8, 16, 128), b(3, 8, 16, 128), b(3, 8, 16, 128), D((6, 8)), D((6, 8))]

def tap_scratch():
    D = pltpu.SemaphoreType.DMA
    return [pltpu.VMEM((n, 16, 512), jnp.float32) for n in (2, 4, 4, 8)] + [D((4,)), D((4,))]

def entry_scratch():
    return [pltpu.SemaphoreType.REGULAR] * 2

def kernel(x_ref, c_ref, taps_ref, mix_ref, o_ref, gt_out, gm_out, *scratch):
    scratch = list(scratch)
    def take(n):
        got = scratch[:n]
        del scratch[:n]
        return got
    ox, sx, rx, oc, sc, rc, og, sg, rg = take(9)
    pair_sems, sems, loc = take(3)
    xf, act, dg, g, gb, lag, gt = take(7)
    gm, *rest = take(11)
    red = Reduction(gm, gm_out, *rest)
    *bufs, tss, trs = take(6)
    taps = TapSums(bufs, tss, trs)
    plane_sem, all_sem = take(2)
    h, w, x, z, c = coords()

    tokens_to_tiles(x_ref, sx, ox, c)
    enter(plane_sem, all_sem)
    px = pair_copy(ox, sx, pair_sems, 0)
    px.start()
    tokens_to_tiles(c_ref, sc, oc, c)
    pc = pair_copy(oc, sc, pair_sems, 1)
    pc.start()
    px.wait_recv()
    spread(sx, rx, sems, loc, 0)
    pc.wait_recv()
    spread(sc, rc, sems, loc, 1)
    xf[:, :, 0:PAD] = jnp.zeros((LEVELS, 4, PAD, 128), jnp.float32)
    lag[:, 512:512 + PAD] = jnp.zeros((4, PAD, 128), jnp.float32)
    gt[...] = jnp.zeros((16, 512), jnp.float32)

    spread_arrived(sx, rx, sems, loc, 0)
    def put_x(i, cg, t):
        xf[0, cg, pl.ds(pl.multiple_of(PAD + i * 64, 32), 64)] = t
    tiles_to_rows(rx, put_x)
    for l in range(LEVELS):
        forward(l, xf, act, dg, taps_ref, mix_ref)

    spread_arrived(sc, rc, sems, loc, 1)
    def put_c(i, cg, t):
        rows = pl.ds(pl.multiple_of(i * 64, 64), 64)
        g[cg, rows] = t
        gb[rows, cg * 128:cg * 128 + 128] = t.astype(jnp.bfloat16)
    tiles_to_rows(rc, put_c)

    for l in reversed(range(LEVELS)):
        gm[l] = mix_grad(l, act, gb).astype(jnp.bfloat16)
        red.halve(l)
        backward(l, xf, dg, g, gb, lag, taps_ref, mix_ref, gt)
        if l == 3:
            red.quarter(5)
        if l == 2:
            red.quarter(4)
            red.sixteenth(5)
        if l == 1:
            red.quarter(3)
            red.sixteenth(4)
        if l == 0:
            red.quarter(2)
            red.tile(2)
            red.sixteenth(3)

    rows_to_tiles(gb, sg, og, c)
    pg = pair_copy(og, sg, pair_sems, 2)
    pg.start()
    taps.send(0, gt[...])
    red.quarter(1)
    red.sixteenth(2)
    pg.wait_recv()
    spread(sg, rg, sems, loc, 2)
    red.quarter(0)
    red.untile(2)
    taps.send(1, taps.total(0))
    red.sixteenth(1)
    red.tile(1)
    red.sixteenth(0)
    taps.send(2, taps.total(1))
    red.unsixteenth(2)
    red.untile(1)
    red.tile(0)
    taps.send(3, taps.total(2))
    red.unquarter(2)
    red.unsixteenth(1)
    red.untile(0)
    gt_out[...] = taps.total(3)
    red.unhalve(2)
    red.unquarter(1)
    red.unsixteenth(0)
    spread_arrived(sg, rg, sems, loc, 2)
    tiles_to_tokens(rg, o_ref)
    red.unhalve(1)
    red.unquarter(0)
    red.unhalve(0)
    for p in (2, 1, 0):
        red.finish(p)
    taps.finish()
    px.wait_send()
    pc.wait_send()
    pg.wait_send()
    for k, (s, r) in enumerate(((sx, rx), (sc, rc), (sg, rg))):
        spread_sent(s, r, sems, k)

def local(inputs, filter_taps, mixing, cotangent):
    f, b = jnp.float32, jnp.bfloat16
    V, S, D = pltpu.VMEM, jax.ShapeDtypeStruct, pltpu.SemaphoreType.DMA
    exchange = [V((64, 16, 128), b), V((64, 2, 16, 128), b), V((64, 2, 16, 128), b)] * 3 + [D((2, 3)), D((2, 3)), D((3,))]
    levels = [V((LEVELS, 4, PAD + 512, 128), f), V((LEVELS, 512, 512), b), V((LEVELS, 4, 512, 128), f), V((4, 512, 128), f), V((512, 512), b), V((4, 512 + PAD, 128), f), V((16, 512), f)]
    o, gt, gm = pl.pallas_call(
        kernel,
        out_shape=[S((512, 512), f), S((16, 512), f), S((LEVELS, 512, 512), b)],
        in_specs=[VM] * 4,
        out_specs=[VM] * 3,
        scratch_shapes=exchange + levels + reduction_scratch() + tap_scratch() + entry_scratch(),
        compiler_params=pltpu.CompilerParams(collective_id=1, has_side_effects=True, vmem_limit_bytes=50 << 20),
        cost_estimate=pl.CostEstimate(flops=4831838208, bytes_accessed=10 << 20, transcendentals=1572864),
    )(inputs[0], cotangent[0], filter_taps, mixing)
    return o[None], gt[:12].reshape(6, 2, 512), gm

def solution(mesh):
    halves = P("dp", "seq", None)
    return jax.shard_map(local, mesh=mesh, in_specs=(halves, P(), P(), halves), out_specs=(halves, P(), P()), check_vma=False)
```

```python
import functools, jax, jax.numpy as jnp
from jax import lax
from jax.sharding import PartitionSpec as P
from jax.experimental import pallas as pl
from jax.experimental.pallas import tpu as pltpu
MESH = pl.DeviceIdType.MESH
CHIPS = 64

def coords():
    me = lax.axis_index("seq")
    c = lax.rem(me, 2)
    z = lax.rem(lax.div(me, 2), 8)
    x = lax.rem(lax.div(me, 16), 4)
    w = lax.div(me, 64)
    h = lax.axis_index("dp")
    return h, w, x, z, c

def place(h, w, x, z, c):
    return {"seq": ((w * 4 + x) * 8 + z) * 2 + c, "dp": h}

def on_y(y, x, z, c):
    return place(lax.div(y, 2), lax.rem(y, 2), x, z, c)

def signal(sem, dev):
    pl.semaphore_signal(sem, inc=1, device_id=dev, device_id_type=MESH)

def greet():
    h, w, x, z, c = coords()
    bar = pltpu.get_barrier_semaphore()
    signal(bar, place(h, w, x, z, 1 - c))
    @pl.loop(1, 8)
    def _(k):
        signal(bar, place(h, w, x, lax.rem(z + k, 8), c))
    @pl.loop(1, 4)
    def _(k):
        signal(bar, place(h, w, lax.rem(x + k, 4), z, c))
    y = h * 2 + w
    @pl.loop(1, 4)
    def _(k):
        signal(bar, on_y(lax.rem(y + k, 4), x, z, c))

def meet(plane_sem):
    h, w, x, z, c = coords()
    pl.semaphore_wait(pltpu.get_barrier_semaphore(), 14)
    @pl.loop(1, 4)
    def _(k):
        signal(plane_sem, place(h, w, lax.rem(x + k, 4), z, c))

def enter(plane_sem, all_sem):
    h, w, x, z, c = coords()
    pl.semaphore_wait(plane_sem, 3)
    signal(all_sem, place(h, 1 - w, x, z, c))
    pl.semaphore_wait(all_sem, 1)

def selection(out_of, shape=(256, 256)):
    o = lax.broadcasted_iota(jnp.int32, shape, 0)
    i = lax.broadcasted_iota(jnp.int32, shape, 1)
    return jnp.where(i == out_of(o), 1.0, 0.0).astype(jnp.bfloat16)

def tokens_to_tiles(a_ref, mine, other, c):
    def src(o):
        half, j, cg, n = o // 128, (o // 16) % 8, (o // 4) % 4, o % 4
        return (n * 4 + cg) * 16 + 2 * j + jnp.where(half == 0, c, 1 - c)
    pm = selection(src)
    @pl.loop(0, 8)
    def _(g):
        m = jnp.concatenate([a_ref[pl.ds(pl.multiple_of(n * 128 + g * 16, 16), 16), cg * 128:(cg + 1) * 128] for n in range(4) for cg in range(4)], axis=0)
        t = jnp.dot(pm, m, preferred_element_type=jnp.float32).astype(jnp.bfloat16).reshape(2, 8, 16, 128)
        mine[pl.ds(g * 8, 8), c] = t[0]
        other[pl.ds(g * 8, 8)] = t[1]

def tiles_to_rows(r_ref, put):
    qm = selection(lambda o: ((o // 4) % 16 * 4 + o // 64) * 4 + o % 4)
    @pl.loop(0, 8)
    def _(g):
        m = r_ref[pl.ds(g * 8, 8)].reshape(256, 128)
        t = jnp.dot(qm, m, preferred_element_type=jnp.float32)
        for cg in range(4):
            put(g, cg, t[cg * 64:(cg + 1) * 64])

def rows_to_tiles(g_ref, mine, other, c):
    def src(o):
        half, j, cg, n = o // 128, (o // 16) % 8, (o // 4) % 4, o % 4
        return (cg * 16 + 2 * j + jnp.where(half == 0, c, 1 - c)) * 4 + n
    pm = selection(src)
    @pl.loop(0, 8)
    def _(g):
        m = jnp.concatenate([g_ref[pl.ds(pl.multiple_of(g * 64, 64), 64), cg * 128:(cg + 1) * 128] for cg in range(4)], axis=0)
        t = jnp.dot(pm, m, preferred_element_type=jnp.float32).astype(jnp.bfloat16).reshape(2, 8, 16, 128)
        mine[pl.ds(g * 8, 8), c] = t[0]
        other[pl.ds(g * 8, 8)] = t[1]

def tiles_to_tokens(r_ref, o_ref):
    qm = selection(lambda o: (o % 16 * 4 + (o // 16) % 4) * 4 + o // 64)
    @pl.loop(0, 8)
    def _(g):
        m = r_ref[pl.ds(g * 8, 8)].reshape(256, 128)
        t = jnp.dot(qm, m, preferred_element_type=jnp.float32)
        for n in range(4):
            for cg in range(4):
                o_ref[pl.ds(pl.multiple_of(n * 128 + g * 16, 16), 16), cg * 128:(cg + 1) * 128] = t[(n * 4 + cg) * 16:(n * 4 + cg + 1) * 16]

def pair_copy(other, s_ref, sems, k):
    h, w, x, z, c = coords()
    return pltpu.make_async_remote_copy(other, s_ref.at[:, c], sems.at[0, k], sems.at[1, k], device_id=place(h, w, x, z, 1 - c), device_id_type=MESH)

def spread(s_ref, r_ref, sems, loc, k, begin=1, end=64):
    h, w, x, z, c = coords()
    j = (w * 4 + x) * 8 + z
    if begin == 1:
        pltpu.make_async_copy(s_ref.at[j], r_ref.at[j], loc.at[k]).start()
    @pl.loop(begin, end)
    def _(t):
        b = lax.rem(t, 8)
        a = lax.div(t, 8)
        dz = jnp.where(lax.rem(b, 2) == 1, lax.div(b + 1, 2), 8 - lax.div(b, 2))
        z2 = lax.rem(z + dz, 8)
        x2 = lax.rem(x + lax.rem(a, 4), 4)
        w2 = lax.rem(w + lax.div(a, 4), 2)
        pltpu.make_async_remote_copy(s_ref.at[(w2 * 4 + x2) * 8 + z2], r_ref.at[j], sems.at[0, k], sems.at[1, k], device_id=place(h, w2, x2, z2, c), device_id_type=MESH).start()

def spread_arrived(s_ref, r_ref, sems, loc, k, begin=1, end=64):
    h, w, x, z, c = coords()
    j = (w * 4 + x) * 8 + z
    if begin == 1:
        pltpu.make_async_copy(s_ref.at[j], r_ref.at[j], loc.at[k]).wait()
    some = pl.ds(0, end - begin)
    pltpu.make_async_copy(s_ref.at[some], r_ref.at[some], sems.at[1, k]).wait()

def spread_sent(s_ref, r_ref, sems, k, begin=1, end=64):
    some = pl.ds(0, end - begin)
    pltpu.make_async_copy(s_ref.at[some], r_ref.at[some], sems.at[0, k]).wait()

LEVELS = 6
K0 = 0.7978845608028654
K1C = K0 * 0.044715
PAD = 32
TILE = 128

def forward(l, xf, act, dg, taps_ref, mix_ref):
    d = 1 << l
    for rt in range(512 // TILE):
        r0 = rt * TILE
        for cg in range(4):
            lanes = slice(cg * 128, cg * 128 + 128)
            cur = xf[l, cg, PAD + r0:PAD + r0 + TILE]
            lag = xf[l, cg, PAD + r0 - d:PAD + r0 - d + TILE]
            p = taps_ref[l, 0:1, lanes] * cur + taps_ref[l, 1:2, lanes] * lag
            p2 = p * p
            t = jnp.tanh(p * (K0 + K1C * p2))
            half = 0.5 + 0.5 * t
            act[l, r0:r0 + TILE, lanes] = (p * half).astype(jnp.bfloat16)
            dg[l, cg, r0:r0 + TILE] = half + (half * (1.0 - half) * p) * (2 * K0 + 6 * K1C * p2)
        if l + 1 < LEVELS:
            m = jnp.dot(act[l, r0:r0 + TILE, :], mix_ref[l], preferred_element_type=jnp.float32)
            for cg in range(4):
                nxt = xf[l, cg, PAD + r0:PAD + r0 + TILE] + m[:, cg * 128:cg * 128 + 128]
                xf[l + 1, cg, PAD + r0:PAD + r0 + TILE] = nxt.astype(jnp.bfloat16).astype(jnp.float32)

def backward(l, xf, dg, g, gb, lag, taps_ref, mix_ref, gtaps):
    d = 1 << l
    sums = [[jnp.zeros((8, 128), jnp.float32) for _ in range(2)] for _ in range(4)]
    for rt in reversed(range(512 // TILE)):
        r0 = rt * TILE
        ga = lax.dot_general(gb[r0:r0 + TILE, :], mix_ref[l], (((1,), (1,)), ((), ())), preferred_element_type=jnp.float32)
        for cg in range(4):
            lanes = slice(cg * 128, cg * 128 + 128)
            gp = ga[:, lanes] * dg[l, cg, r0:r0 + TILE]
            cur = xf[l, cg, PAD + r0:PAD + r0 + TILE]
            old = xf[l, cg, PAD + r0 - d:PAD + r0 - d + TILE]
            sums[cg][0] += jnp.sum((gp * cur).reshape(TILE // 8, 8, 128), axis=0)
            sums[cg][1] += jnp.sum((gp * old).reshape(TILE // 8, 8, 128), axis=0)
            lag[cg, r0:r0 + TILE] = (taps_ref[l, 1:2, lanes] * gp).astype(jnp.bfloat16).astype(jnp.float32)
            new = g[cg, r0:r0 + TILE] + taps_ref[l, 0:1, lanes] * gp + lag[cg, r0 + d:r0 + d + TILE]
            g[cg, r0:r0 + TILE] = new
            gb[r0:r0 + TILE, lanes] = new.astype(jnp.bfloat16)
    for cg in range(4):
        for k in range(2):
            gtaps[2 * l + k:2 * l + k + 1, cg * 128:cg * 128 + 128] = jnp.sum(sums[cg][k], axis=0, keepdims=True)

def mix_grad(l, act, gb):
    return lax.dot_general(act[l], gb[...], (((0,), (0,)), ((), ())), preferred_element_type=jnp.float32)


VM = pl.BlockSpec(memory_space=pltpu.VMEM)

class Reduction:
    def __init__(self, gm, final, out, c0, hh, r1, qq, r2, e8, r3, f8, ss, rs, ls):
        self.__dict__.update(gm=gm, final=final, out=out, ls=ls, c0=c0, hh=hh, r1=r1, qq=qq, r2=r2, e8=e8, r3=r3, f8=f8, ss=ss, rs=rs)
        self.h, self.w, self.x, self.z, self.c = h, w, x, z, c = coords()
        self.y = h * 2 + w
        others = lambda i, n: [lax.rem(i + k, n) for k in range(1, n)]
        self.on_axis = {1: [(j, place(h, w, j, z, c)) for j in others(x, 4)], 0: [(j, on_y(j, x, z, c)) for j in others(self.y, 4)]}
        self.on_z = [(j, place(h, w, x, j, c)) for j in others(z, 8)]

    def first(self, l):
        return self.x if l % 2 else self.y

    def second(self, l):
        return self.y if l % 2 else self.x

    def copy(self, src, dst, l, stage, dev):
        return pltpu.make_async_remote_copy(src, dst, self.ss.at[l, stage], self.rs.at[l, stage], device_id=dev, device_id_type=MESH)

    def other_core(self):
        return place(self.h, self.w, self.x, self.z, 1 - self.c)

    def rows(self, l):
        r256 = self.c * 256
        r64 = r256 + self.first(l) * 64
        return pl.multiple_of(r256, 256), pl.multiple_of(r64, 64), pl.multiple_of(r64 + self.second(l) * 16, 16)

    def took(self, ref, l, stage):
        pltpu.make_async_copy(ref, ref, self.rs.at[l, stage]).wait()

    def gave(self, ref, l, stage):
        pltpu.make_async_copy(ref, ref, self.ss.at[l, stage]).wait()

    def halve(self, l):
        far = pl.multiple_of((1 - self.c) * 256, 256)
        self.copy(self.gm.at[l, pl.ds(far, 256)], self.c0.at[l], l, 0, self.other_core()).start()

    def quarter(self, l):
        self.took(self.c0.at[l], l, 0)
        near = self.rows(l)[0]
        self.hh[l] = (self.gm[l, pl.ds(near, 256)].astype(jnp.float32) + self.c0[l].astype(jnp.float32)).astype(jnp.bfloat16)
        i = self.first(l)
        for j, dev in self.on_axis[l % 2]:
            self.copy(self.hh.at[l, pl.ds(pl.multiple_of(j * 64, 64), 64)], self.r1.at[l, i], l, 1, dev).start()

    def sixteenth(self, l):
        self.took(self.r1.at[l, pl.ds(0, 3)], l, 1)
        i = self.first(l)
        s = self.hh[l, pl.ds(pl.multiple_of(i * 64, 64), 64)].astype(jnp.float32)
        for k in range(1, 4):
            s += self.r1[l, lax.rem(i + k, 4)].astype(jnp.float32)
        self.qq[l] = s.astype(jnp.bfloat16)
        i2 = self.second(l)
        for j, dev in self.on_axis[1 - l % 2]:
            self.copy(self.qq.at[l, pl.ds(pl.multiple_of(j * 16, 16), 16)], self.r2.at[l, i2], l, 2, dev).start()

    def tile(self, p):
        z = self.z
        for l in (2 * p, 2 * p + 1):
            self.took(self.r2.at[l, pl.ds(0, 3)], l, 2)
            i2 = self.second(l)
            s = self.qq[l, pl.ds(pl.multiple_of(i2 * 16, 16), 16)].astype(jnp.float32)
            for k in range(1, 4):
                s += self.r2[l, lax.rem(i2 + k, 4)].astype(jnp.float32)
            for cg in range(4):
                self.e8[p, l % 2 * 4 + cg] = s[:, cg * 128:cg * 128 + 128].astype(jnp.bfloat16)
        for j, dev in self.on_z:
            self.copy(self.e8.at[p, j], self.r3.at[p, z], 2 * p, 3, dev).start()

    def untile(self, p):
        z = self.z
        self.took(self.r3.at[p, pl.ds(0, 7)], 2 * p, 3)
        s = self.e8[p, z].astype(jnp.float32)
        for k in range(1, 8):
            s += self.r3[p, lax.rem(z + k, 8)].astype(jnp.float32)
        self.f8[p, z] = s.astype(jnp.bfloat16)
        for j, dev in self.on_z:
            self.copy(self.f8.at[p, z], self.f8.at[p, z], 2 * p, 4, dev).start()

    def unsixteenth(self, p):
        self.took(self.f8.at[p, pl.ds(0, 7)], 2 * p, 4)
        for l in (2 * p, 2 * p + 1):
            r16 = self.rows(l)[2]
            for cg in range(4):
                self.out[l, pl.ds(r16, 16), cg * 128:cg * 128 + 128] = self.f8[p, l % 2 * 4 + cg]
            mine = self.out.at[l, pl.ds(r16, 16)]
            for j, dev in self.on_axis[1 - l % 2]:
                self.copy(mine, mine, l, 5, dev).start()

    def unquarter(self, p):
        for l in (2 * p, 2 * p + 1):
            self.took(self.out.at[l, pl.ds(0, 48)], l, 5)
            mine = self.out.at[l, pl.ds(self.rows(l)[1], 64)]
            for j, dev in self.on_axis[l % 2]:
                self.copy(mine, mine, l, 6, dev).start()

    def unhalve(self, p):
        for l in (2 * p, 2 * p + 1):
            self.took(self.out.at[l, pl.ds(0, 192)], l, 6)
            mine = self.out.at[l, pl.ds(self.rows(l)[0], 256)]
            there = self.final.at[l, pl.ds(self.rows(l)[0], 256)]
            self.copy(mine, there, l, 7, self.other_core()).start()
            pltpu.make_async_copy(mine, there, self.ls.at[l]).start()

    def finish(self, p):
        for l in (2 * p, 2 * p + 1):
            half = self.final.at[l, pl.ds(0, 256)]
            self.took(half, l, 7)
            pltpu.make_async_copy(half, half, self.ls.at[l]).wait()
            self.gave(self.c0.at[l], l, 0)
            self.gave(self.r1.at[l, pl.ds(0, 3)], l, 1)
            self.gave(self.r2.at[l, pl.ds(0, 3)], l, 2)
            self.gave(self.out.at[l, pl.ds(0, 48)], l, 5)
            self.gave(self.out.at[l, pl.ds(0, 192)], l, 6)
            self.gave(self.out.at[l, pl.ds(0, 256)], l, 7)
        self.gave(self.r3.at[p, pl.ds(0, 7)], 2 * p, 3)
        self.gave(self.f8.at[p, pl.ds(0, 7)], 2 * p, 4)

class TapSums:
    def __init__(self, bufs, ss, rs):
        self.bufs, self.ss, self.rs = bufs, ss, rs
        self.h, self.w, self.x, self.z, self.c = coords()
        self.at = (self.c, self.x, self.h * 2 + self.w, self.z)
        self.size = (2, 4, 4, 8)

    def dev(self, stage, j):
        if stage == 0:
            return place(self.h, self.w, self.x, self.z, j)
        if stage == 1:
            return place(self.h, self.w, j, self.z, self.c)
        if stage == 2:
            return on_y(j, self.x, self.z, self.c)
        return place(self.h, self.w, self.x, j, self.c)

    def send(self, stage, value):
        n, i, buf = self.size[stage], self.at[stage], self.bufs[stage]
        buf[i] = value
        @pl.loop(1, n)
        def _(k):
            pltpu.make_async_remote_copy(buf.at[i], buf.at[i], self.ss.at[stage], self.rs.at[stage],
                device_id=self.dev(stage, lax.rem(i + k, n)), device_id_type=MESH).start()

    def total(self, stage):
        n, buf = self.size[stage], self.bufs[stage]
        part = buf.at[pl.ds(0, n - 1)]
        pltpu.make_async_copy(part, part, self.rs.at[stage]).wait()
        s = buf[0]
        for k in range(1, n):
            s += buf[k]
        return s

    def finish(self):
        for stage in range(4):
            part = self.bufs[stage].at[pl.ds(0, self.size[stage] - 1)]
            pltpu.make_async_copy(part, part, self.ss.at[stage]).wait()

def reduction_scratch():
    b = lambda *s: pltpu.VMEM(s, jnp.bfloat16)
    D = pltpu.SemaphoreType.DMA
    return [b(6, 512, 512), b(6, 512, 512), b(6, 256, 512), b(6, 256, 512), b(6, 4, 64, 512), b(6, 64, 512), b(6, 4, 16, 512), b(3, 8, 16, 128), b(3, 8, 16, 128), b(3, 8, 16, 128), D((6, 8)), D((6, 8)), D((6,))]

def tap_scratch():
    D = pltpu.SemaphoreType.DMA
    return [pltpu.VMEM((n, 16, 512), jnp.float32) for n in (2, 4, 4, 8)] + [D((4,)), D((4,))]

def entry_scratch():
    return [pltpu.SemaphoreType.REGULAR] * 2

FIRST = 40

def kernel(x_hbm, c_hbm, taps_ref, mix_hbm, rg, gt_out, gm_out, *scratch):
    scratch = list(scratch)
    def take(n):
        got = scratch[:n]
        del scratch[:n]
        return got
    x_ref, c_ref, mix_ref, in_sems = take(4)
    ox, sx, rx, oc, sc, rc, og, sg = take(8)
    pair_sems, sems, loc = take(3)
    xf, act, dg, g, gb, lag, gt = take(7)
    gm, *rest = take(13)
    red = Reduction(gm, gm_out, *rest)
    *bufs, tss, trs = take(6)
    taps = TapSums(bufs, tss, trs)
    plane_sem, all_sem = take(2)
    h, w, x, z, c = coords()

    greet()
    loads = [pltpu.make_async_copy(s, d, in_sems.at[i]) for i, (s, d) in enumerate(((x_hbm, x_ref), (c_hbm, c_ref), (mix_hbm, mix_ref)))]
    for load in loads:
        load.start()
    xf[:, :, 0:PAD] = jnp.zeros((LEVELS, 4, PAD, 128), jnp.float32)
    lag[:, 512:512 + PAD] = jnp.zeros((4, PAD, 128), jnp.float32)
    gt[...] = jnp.zeros((16, 512), jnp.float32)
    meet(plane_sem)
    loads[0].wait()
    tokens_to_tiles(x_ref, sx, ox, c)
    enter(plane_sem, all_sem)
    px = pair_copy(ox, sx, pair_sems, 0)
    px.start()
    loads[1].wait()
    tokens_to_tiles(c_ref, sc, oc, c)
    pc = pair_copy(oc, sc, pair_sems, 1)
    pc.start()
    px.wait_recv()
    spread(sx, rx, sems, loc, 0, 1, FIRST)
    spread(sx, rx, sems, loc, 3, FIRST, 64)
    loads[2].wait()
    pc.wait_recv()
    spread_arrived(sx, rx, sems, loc, 0, 1, FIRST)
    spread(sc, rc, sems, loc, 1)

    spread_arrived(sx, rx, sems, loc, 3, FIRST, 64)
    def put_x(i, cg, t):
        xf[0, cg, pl.ds(pl.multiple_of(PAD + i * 64, 32), 64)] = t
    tiles_to_rows(rx, put_x)
    for l in range(LEVELS):
        forward(l, xf, act, dg, taps_ref, mix_ref)

    spread_arrived(sc, rc, sems, loc, 1)
    def put_c(i, cg, t):
        rows = pl.ds(pl.multiple_of(i * 64, 64), 64)
        g[cg, rows] = t
        gb[rows, cg * 128:cg * 128 + 128] = t.astype(jnp.bfloat16)
    tiles_to_rows(rc, put_c)

    for l in reversed(range(LEVELS)):
        gm[l] = mix_grad(l, act, gb).astype(jnp.bfloat16)
        red.halve(l)
        backward(l, xf, dg, g, gb, lag, taps_ref, mix_ref, gt)
        if l == 3:
            red.quarter(5)
        if l == 2:
            red.quarter(4)
        if l == 1:
            red.quarter(3)
        if l == 0:
            red.quarter(2)
            red.sixteenth(5)

    rows_to_tiles(gb, sg, og, c)
    pg = pair_copy(og, sg, pair_sems, 2)
    pg.start()
    taps.send(0, gt[...])
    red.sixteenth(4)
    red.quarter(1)
    pg.wait_recv()
    spread(sg, rg, sems, loc, 2, 1, 8)
    red.quarter(0)
    red.sixteenth(3)
    red.sixteenth(2)
    red.tile(2)
    taps.send(1, taps.total(0))
    spread(sg, rg, sems, loc, 2, 8, 16)
    red.sixteenth(1)
    red.sixteenth(0)
    red.untile(2)
    taps.send(2, taps.total(1))
    spread(sg, rg, sems, loc, 2, 16, 24)
    red.tile(1)
    red.tile(0)
    spread(sg, rg, sems, loc, 2, 24, 32)
    red.unsixteenth(2)
    taps.send(3, taps.total(2))
    spread(sg, rg, sems, loc, 2, 32, 40)
    red.untile(1)
    red.untile(0)
    spread(sg, rg, sems, loc, 2, 40, 48)
    red.unquarter(2)
    spread(sg, rg, sems, loc, 2, 48, 56)
    red.unsixteenth(1)
    red.unsixteenth(0)
    spread(sg, rg, sems, loc, 2, 56, 64)
    gt_out[...] = taps.total(3)
    red.unquarter(1)
    red.unquarter(0)
    red.unhalve(2)
    red.unhalve(1)
    red.unhalve(0)
    spread_arrived(sg, rg, sems, loc, 2)
    for p in (2, 1, 0):
        red.finish(p)
    taps.finish()
    px.wait_send()
    pc.wait_send()
    pg.wait_send()
    spread_sent(sx, rx, sems, 0, 1, FIRST)
    spread_sent(sx, rx, sems, 3, FIRST, 64)
    spread_sent(sc, rc, sems, 1)
    spread_sent(sg, rg, sems, 2)

def finish(rg_hbm, gt, gm, o_hbm, gt_out, gm_out, rg, o_ref, held, sems, o_sem):
    ins = [pltpu.make_async_copy(gm.at[l], held.at[l], sems.at[0, l]) for l in range(LEVELS)]
    outs = [pltpu.make_async_copy(held.at[l], gm_out.at[l], sems.at[1, l]) for l in range(LEVELS)]
    tiles = pltpu.make_async_copy(rg_hbm, rg, o_sem)
    tiles.start()
    for move in ins:
        move.start()
    for l in range(LEVELS):
        gt_out[l] = gt[2 * l:2 * l + 2]
    tiles.wait()
    tiles_to_tokens(rg, o_ref)
    tokens = pltpu.make_async_copy(o_ref, o_hbm, o_sem)
    tokens.start()
    for l in range(LEVELS):
        ins[l].wait()
        outs[l].start()
    for move in outs:
        move.wait()
    tokens.wait()

def local(inputs, filter_taps, mixing, cotangent):
    f, b = jnp.float32, jnp.bfloat16
    V, S, D = pltpu.VMEM, jax.ShapeDtypeStruct, pltpu.SemaphoreType.DMA
    ANY = pl.BlockSpec(memory_space=pl.ANY)
    loaded = [V((512, 512), b), V((512, 512), b), V((LEVELS, 512, 512), b), D((3,))]
    exchange = ([V((64, 16, 128), b), V((64, 2, 16, 128), b), V((64, 2, 16, 128), b)] * 3)[:-1] + [D((2, 3)), D((2, 4)), D((4,))]
    levels = [V((LEVELS, 4, PAD + 512, 128), f), V((LEVELS, 512, 512), b), V((LEVELS, 4, 512, 128), f), V((4, 512, 128), f), V((512, 512), b), V((4, 512 + PAD, 128), f), V((16, 512), f)]
    rg, gt, gm = pl.pallas_call(
        kernel,
        out_shape=[S((64, 2, 16, 128), b), S((16, 512), f), S((LEVELS, 512, 512), b)],
        in_specs=[ANY, ANY, VM, ANY],
        out_specs=[ANY, VM, ANY],
        scratch_shapes=loaded + exchange + levels + reduction_scratch() + tap_scratch() + entry_scratch(),
        compiler_params=pltpu.CompilerParams(collective_id=1, has_side_effects=True, vmem_limit_bytes=60 << 20),
        cost_estimate=pl.CostEstimate(flops=4831838208, bytes_accessed=10 << 20, transcendentals=1572864),
    )(inputs[0], cotangent[0], filter_taps, mixing)
    o, gt, gm = pl.pallas_call(
        finish,
        out_shape=[S((512, 512), f), S((LEVELS, 2, 512), f), S((LEVELS, 512, 512), b)],
        in_specs=[ANY, VM, ANY],
        out_specs=[ANY, VM, ANY],
        scratch_shapes=[V((64, 2, 16, 128), b), V((512, 512), f), V((LEVELS, 512, 512), b), D((2, LEVELS)), D],
        compiler_params=pltpu.CompilerParams(vmem_limit_bytes=60 << 20),
    )(rg, gt, gm)
    return o[None], gt, gm

def solution(mesh):
    halves = P("dp", "seq", None)
    return jax.shard_map(local, mesh=mesh, in_specs=(halves, P(), P(), halves), out_specs=(halves, P(), P()), check_vma=False)
```

```python
import functools, jax, jax.numpy as jnp
from jax import lax
from jax.sharding import PartitionSpec as P
from jax.experimental import pallas as pl
from jax.experimental.pallas import tpu as pltpu
MESH = pl.DeviceIdType.MESH
CHIPS = 64

def coords():
    me = lax.axis_index("seq")
    c = lax.rem(me, 2)
    z = lax.rem(lax.div(me, 2), 8)
    x = lax.rem(lax.div(me, 16), 4)
    w = lax.div(me, 64)
    h = lax.axis_index("dp")
    return h, w, x, z, c

def place(h, w, x, z, c):
    return {"seq": ((w * 4 + x) * 8 + z) * 2 + c, "dp": h}

def on_y(y, x, z, c):
    return place(lax.div(y, 2), lax.rem(y, 2), x, z, c)

def signal(sem, dev):
    pl.semaphore_signal(sem, inc=1, device_id=dev, device_id_type=MESH)

def greet():
    h, w, x, z, c = coords()
    bar = pltpu.get_barrier_semaphore()
    signal(bar, place(h, w, x, z, 1 - c))
    @pl.loop(1, 8)
    def _(k):
        signal(bar, place(h, w, x, lax.rem(z + k, 8), c))
    @pl.loop(1, 4)
    def _(k):
        signal(bar, place(h, w, lax.rem(x + k, 4), z, c))
    y = h * 2 + w
    @pl.loop(1, 4)
    def _(k):
        signal(bar, on_y(lax.rem(y + k, 4), x, z, c))

def meet(plane_sem):
    h, w, x, z, c = coords()
    pl.semaphore_wait(pltpu.get_barrier_semaphore(), 14)
    @pl.loop(1, 4)
    def _(k):
        signal(plane_sem, place(h, w, lax.rem(x + k, 4), z, c))

def enter(plane_sem, all_sem):
    h, w, x, z, c = coords()
    pl.semaphore_wait(plane_sem, 3)
    signal(all_sem, place(h, 1 - w, x, z, c))
    pl.semaphore_wait(all_sem, 1)

def selection(out_of, shape=(256, 256)):
    o = lax.broadcasted_iota(jnp.int32, shape, 0)
    i = lax.broadcasted_iota(jnp.int32, shape, 1)
    return jnp.where(i == out_of(o), 1.0, 0.0).astype(jnp.bfloat16)

def tokens_to_tiles(a_ref, mine, other, c):
    def src(o):
        half, j, cg, n = o // 128, (o // 16) % 8, (o // 4) % 4, o % 4
        return (n * 4 + cg) * 16 + 2 * j + jnp.where(half == 0, c, 1 - c)
    pm = selection(src)
    @pl.loop(0, 8)
    def _(g):
        m = jnp.concatenate([a_ref[pl.ds(pl.multiple_of(n * 128 + g * 16, 16), 16), cg * 128:(cg + 1) * 128] for n in range(4) for cg in range(4)], axis=0)
        t = jnp.dot(pm, m, preferred_element_type=jnp.float32).astype(jnp.bfloat16).reshape(2, 8, 16, 128)
        mine[pl.ds(g * 8, 8), c] = t[0]
        other[pl.ds(g * 8, 8)] = t[1]

def tiles_to_rows(r_ref, put):
    qm = selection(lambda o: ((o // 4) % 16 * 4 + o // 64) * 4 + o % 4)
    @pl.loop(0, 8)
    def _(g):
        m = r_ref[pl.ds(g * 8, 8)].reshape(256, 128)
        t = jnp.dot(qm, m, preferred_element_type=jnp.float32)
        for cg in range(4):
            put(g, cg, t[cg * 64:(cg + 1) * 64])

def rows_to_tiles(g_ref, mine, other, c):
    def src(o):
        half, j, cg, n = o // 128, (o // 16) % 8, (o // 4) % 4, o % 4
        return (cg * 16 + 2 * j + jnp.where(half == 0, c, 1 - c)) * 4 + n
    pm = selection(src)
    @pl.loop(0, 8)
    def _(g):
        m = jnp.concatenate([g_ref[pl.ds(pl.multiple_of(g * 64, 64), 64), cg * 128:(cg + 1) * 128] for cg in range(4)], axis=0)
        t = jnp.dot(pm, m, preferred_element_type=jnp.float32).astype(jnp.bfloat16).reshape(2, 8, 16, 128)
        mine[pl.ds(g * 8, 8), c] = t[0]
        other[pl.ds(g * 8, 8)] = t[1]

def tiles_to_tokens(r_ref, o_ref):
    qm = selection(lambda o: (o % 16 * 4 + (o // 16) % 4) * 4 + o // 64)
    @pl.loop(0, 8)
    def _(g):
        m = r_ref[pl.ds(g * 8, 8)].reshape(256, 128)
        t = jnp.dot(qm, m, preferred_element_type=jnp.float32)
        for n in range(4):
            for cg in range(4):
                o_ref[pl.ds(pl.multiple_of(n * 128 + g * 16, 16), 16), cg * 128:(cg + 1) * 128] = t[(n * 4 + cg) * 16:(n * 4 + cg + 1) * 16]

def pair_copy(other, s_ref, sems, k):
    h, w, x, z, c = coords()
    return pltpu.make_async_remote_copy(other, s_ref.at[:, c], sems.at[0, k], sems.at[1, k], device_id=place(h, w, x, z, 1 - c), device_id_type=MESH)

def spread(s_ref, r_ref, sems, loc, k, begin=1, end=64):
    h, w, x, z, c = coords()
    j = (w * 4 + x) * 8 + z
    if begin == 1:
        pltpu.make_async_copy(s_ref.at[j], r_ref.at[j], loc.at[k]).start()
    @pl.loop(begin, end)
    def _(t):
        b = lax.rem(t, 8)
        a = lax.div(t, 8)
        dz = jnp.where(lax.rem(b, 2) == 1, lax.div(b + 1, 2), 8 - lax.div(b, 2))
        z2 = lax.rem(z + dz, 8)
        x2 = lax.rem(x + lax.rem(a, 4), 4)
        w2 = lax.rem(w + lax.div(a, 4), 2)
        pltpu.make_async_remote_copy(s_ref.at[(w2 * 4 + x2) * 8 + z2], r_ref.at[j], sems.at[0, k], sems.at[1, k], device_id=place(h, w2, x2, z2, c), device_id_type=MESH).start()

def spread_one(s_ref, r_ref, sems, loc, k, core):
    h, w, x, z, c = coords()
    j = (w * 4 + x) * 8 + z
    pltpu.make_async_copy(s_ref.at[j, core], r_ref.at[j, core], loc.at[k]).start()
    @pl.loop(1, 64)
    def _(t):
        b = lax.rem(t, 8)
        a = lax.div(t, 8)
        dz = jnp.where(lax.rem(b, 2) == 1, lax.div(b + 1, 2), 8 - lax.div(b, 2))
        z2 = lax.rem(z + dz, 8)
        x2 = lax.rem(x + lax.rem(a, 4), 4)
        w2 = lax.rem(w + lax.div(a, 4), 2)
        pltpu.make_async_remote_copy(s_ref.at[(w2 * 4 + x2) * 8 + z2, core], r_ref.at[j, core], sems.at[0, k], sems.at[1, k], device_id=place(h, w2, x2, z2, c), device_id_type=MESH).start()

def one_arrived(s_ref, r_ref, sems, loc, k):
    h, w, x, z, c = coords()
    j = (w * 4 + x) * 8 + z
    pltpu.make_async_copy(s_ref.at[j, 0], r_ref.at[j, 0], loc.at[k]).wait()
    some = pl.ds(0, 63)
    pltpu.make_async_copy(s_ref.at[some, 0], r_ref.at[some, 0], sems.at[1, k]).wait()

def one_sent(s_ref, r_ref, sems, k):
    some = pl.ds(0, 63)
    pltpu.make_async_copy(s_ref.at[some, 0], r_ref.at[some, 0], sems.at[0, k]).wait()

def spread_arrived(s_ref, r_ref, sems, loc, k, begin=1, end=64):
    h, w, x, z, c = coords()
    j = (w * 4 + x) * 8 + z
    if begin == 1:
        pltpu.make_async_copy(s_ref.at[j], r_ref.at[j], loc.at[k]).wait()
    some = pl.ds(0, end - begin)
    pltpu.make_async_copy(s_ref.at[some], r_ref.at[some], sems.at[1, k]).wait()

def spread_sent(s_ref, r_ref, sems, k, begin=1, end=64):
    some = pl.ds(0, end - begin)
    pltpu.make_async_copy(s_ref.at[some], r_ref.at[some], sems.at[0, k]).wait()

LEVELS = 6
K0 = 0.7978845608028654
K1C = K0 * 0.044715
PAD = 32
TILE = 128

def forward(l, xf, act, dg, taps_ref, mix_ref):
    d = 1 << l
    for rt in range(512 // TILE):
        r0 = rt * TILE
        for cg in range(4):
            lanes = slice(cg * 128, cg * 128 + 128)
            cur = xf[l, cg, PAD + r0:PAD + r0 + TILE]
            lag = xf[l, cg, PAD + r0 - d:PAD + r0 - d + TILE]
            p = taps_ref[l, 0:1, lanes] * cur + taps_ref[l, 1:2, lanes] * lag
            p2 = p * p
            t = jnp.tanh(p * (K0 + K1C * p2))
            half = 0.5 + 0.5 * t
            act[l, r0:r0 + TILE, lanes] = (p * half).astype(jnp.bfloat16)
            dg[l, cg, r0:r0 + TILE] = half + (half * (1.0 - half) * p) * (2 * K0 + 6 * K1C * p2)
        if l + 1 < LEVELS:
            m = jnp.dot(act[l, r0:r0 + TILE, :], mix_ref[l], preferred_element_type=jnp.float32)
            for cg in range(4):
                nxt = xf[l, cg, PAD + r0:PAD + r0 + TILE] + m[:, cg * 128:cg * 128 + 128]
                xf[l + 1, cg, PAD + r0:PAD + r0 + TILE] = nxt.astype(jnp.bfloat16).astype(jnp.float32)

def backward(l, xf, dg, g, gb, lag, taps_ref, mix_ref, gtaps):
    d = 1 << l
    sums = [[jnp.zeros((8, 128), jnp.float32) for _ in range(2)] for _ in range(4)]
    for rt in reversed(range(512 // TILE)):
        r0 = rt * TILE
        ga = lax.dot_general(gb[r0:r0 + TILE, :], mix_ref[l], (((1,), (1,)), ((), ())), preferred_element_type=jnp.float32)
        for cg in range(4):
            lanes = slice(cg * 128, cg * 128 + 128)
            gp = ga[:, lanes] * dg[l, cg, r0:r0 + TILE]
            cur = xf[l, cg, PAD + r0:PAD + r0 + TILE]
            old = xf[l, cg, PAD + r0 - d:PAD + r0 - d + TILE]
            sums[cg][0] += jnp.sum((gp * cur).reshape(TILE // 8, 8, 128), axis=0)
            sums[cg][1] += jnp.sum((gp * old).reshape(TILE // 8, 8, 128), axis=0)
            lag[cg, r0:r0 + TILE] = (taps_ref[l, 1:2, lanes] * gp).astype(jnp.bfloat16).astype(jnp.float32)
            new = g[cg, r0:r0 + TILE] + taps_ref[l, 0:1, lanes] * gp + lag[cg, r0 + d:r0 + d + TILE]
            g[cg, r0:r0 + TILE] = new
            gb[r0:r0 + TILE, lanes] = new.astype(jnp.bfloat16)
    for cg in range(4):
        for k in range(2):
            gtaps[2 * l + k:2 * l + k + 1, cg * 128:cg * 128 + 128] = jnp.sum(sums[cg][k], axis=0, keepdims=True)

def mix_grad(l, act, gb):
    return lax.dot_general(act[l], gb[...], (((0,), (0,)), ((), ())), preferred_element_type=jnp.float32)


VM = pl.BlockSpec(memory_space=pltpu.VMEM)

class Reduction:
    def __init__(self, gm, final, out, c0, hh, r1, qq, r2, e8, r3, f8, ss, rs, ls):
        self.__dict__.update(gm=gm, final=final, out=out, ls=ls, c0=c0, hh=hh, r1=r1, qq=qq, r2=r2, e8=e8, r3=r3, f8=f8, ss=ss, rs=rs)
        self.h, self.w, self.x, self.z, self.c = h, w, x, z, c = coords()
        self.y = h * 2 + w
        others = lambda i, n: [lax.rem(i + k, n) for k in range(1, n)]
        self.on_axis = {1: [(j, place(h, w, j, z, c)) for j in others(x, 4)], 0: [(j, on_y(j, x, z, c)) for j in others(self.y, 4)]}
        self.on_z = [(j, place(h, w, x, j, c)) for j in others(z, 8)]

    def first(self, l):
        return self.x if l % 2 else self.y

    def second(self, l):
        return self.y if l % 2 else self.x

    def copy(self, src, dst, l, stage, dev):
        return pltpu.make_async_remote_copy(src, dst, self.ss.at[l, stage], self.rs.at[l, stage], device_id=dev, device_id_type=MESH)

    def other_core(self):
        return place(self.h, self.w, self.x, self.z, 1 - self.c)

    def rows(self, l):
        r256 = self.c * 256
        r64 = r256 + self.first(l) * 64
        return pl.multiple_of(r256, 256), pl.multiple_of(r64, 64), pl.multiple_of(r64 + self.second(l) * 16, 16)

    def took(self, ref, l, stage):
        pltpu.make_async_copy(ref, ref, self.rs.at[l, stage]).wait()

    def gave(self, ref, l, stage):
        pltpu.make_async_copy(ref, ref, self.ss.at[l, stage]).wait()

    def halve(self, l):
        far = pl.multiple_of((1 - self.c) * 256, 256)
        self.copy(self.gm.at[l, pl.ds(far, 256)], self.c0.at[l], l, 0, self.other_core()).start()

    def quarter(self, l):
        self.took(self.c0.at[l], l, 0)
        near = self.rows(l)[0]
        self.hh[l] = (self.gm[l, pl.ds(near, 256)].astype(jnp.float32) + self.c0[l].astype(jnp.float32)).astype(jnp.bfloat16)
        i = self.first(l)
        for j, dev in self.on_axis[l % 2]:
            self.copy(self.hh.at[l, pl.ds(pl.multiple_of(j * 64, 64), 64)], self.r1.at[l, i], l, 1, dev).start()

    def sixteenth(self, l):
        self.took(self.r1.at[l, pl.ds(0, 3)], l, 1)
        i = self.first(l)
        s = self.hh[l, pl.ds(pl.multiple_of(i * 64, 64), 64)].astype(jnp.float32)
        for k in range(1, 4):
            s += self.r1[l, lax.rem(i + k, 4)].astype(jnp.float32)
        self.qq[l] = s.astype(jnp.bfloat16)
        i2 = self.second(l)
        for j, dev in self.on_axis[1 - l % 2]:
            self.copy(self.qq.at[l, pl.ds(pl.multiple_of(j * 16, 16), 16)], self.r2.at[l, i2], l, 2, dev).start()

    def tile(self, p):
        z = self.z
        for l in (2 * p, 2 * p + 1):
            self.took(self.r2.at[l, pl.ds(0, 3)], l, 2)
            i2 = self.second(l)
            s = self.qq[l, pl.ds(pl.multiple_of(i2 * 16, 16), 16)].astype(jnp.float32)
            for k in range(1, 4):
                s += self.r2[l, lax.rem(i2 + k, 4)].astype(jnp.float32)
            for cg in range(4):
                self.e8[p, l % 2 * 4 + cg] = s[:, cg * 128:cg * 128 + 128].astype(jnp.bfloat16)
        for j, dev in self.on_z:
            self.copy(self.e8.at[p, j], self.r3.at[p, z], 2 * p, 3, dev).start()

    def untile(self, p):
        z = self.z
        self.took(self.r3.at[p, pl.ds(0, 7)], 2 * p, 3)
        s = self.e8[p, z].astype(jnp.float32)
        for k in range(1, 8):
            s += self.r3[p, lax.rem(z + k, 8)].astype(jnp.float32)
        self.f8[p, z] = s.astype(jnp.bfloat16)
        for j, dev in self.on_z:
            self.copy(self.f8.at[p, z], self.f8.at[p, z], 2 * p, 4, dev).start()

    def unsixteenth(self, p):
        self.took(self.f8.at[p, pl.ds(0, 7)], 2 * p, 4)
        for l in (2 * p, 2 * p + 1):
            r16 = self.rows(l)[2]
            for cg in range(4):
                self.out[l, pl.ds(r16, 16), cg * 128:cg * 128 + 128] = self.f8[p, l % 2 * 4 + cg]
            mine = self.out.at[l, pl.ds(r16, 16)]
            for j, dev in self.on_axis[1 - l % 2]:
                self.copy(mine, mine, l, 5, dev).start()

    def unquarter(self, p):
        for l in (2 * p, 2 * p + 1):
            self.took(self.out.at[l, pl.ds(0, 48)], l, 5)
            mine = self.out.at[l, pl.ds(self.rows(l)[1], 64)]
            for j, dev in self.on_axis[l % 2]:
                self.copy(mine, mine, l, 6, dev).start()

    def unhalve(self, p):
        for l in (2 * p, 2 * p + 1):
            self.took(self.out.at[l, pl.ds(0, 192)], l, 6)
            mine = self.out.at[l, pl.ds(self.rows(l)[0], 256)]
            there = self.final.at[l, pl.ds(self.rows(l)[0], 256)]
            self.copy(mine, there, l, 7, self.other_core()).start()
            pltpu.make_async_copy(mine, there, self.ls.at[l]).start()

    def finish(self, p):
        for l in (2 * p, 2 * p + 1):
            half = self.final.at[l, pl.ds(0, 256)]
            self.took(half, l, 7)
            pltpu.make_async_copy(half, half, self.ls.at[l]).wait()
            self.gave(self.c0.at[l], l, 0)
            self.gave(self.r1.at[l, pl.ds(0, 3)], l, 1)
            self.gave(self.r2.at[l, pl.ds(0, 3)], l, 2)
            self.gave(self.out.at[l, pl.ds(0, 48)], l, 5)
            self.gave(self.out.at[l, pl.ds(0, 192)], l, 6)
            self.gave(self.out.at[l, pl.ds(0, 256)], l, 7)
        self.gave(self.r3.at[p, pl.ds(0, 7)], 2 * p, 3)
        self.gave(self.f8.at[p, pl.ds(0, 7)], 2 * p, 4)

class TapSums:
    def __init__(self, bufs, ss, rs):
        self.pair, self.quarters, *self.slots, self.done = bufs
        self.ss, self.rs = ss, rs
        self.h, self.w, self.x, self.z, self.c = coords()
        self.y = self.h * 2 + self.w

    def others(self, stage):
        h, w, x, z, c = self.h, self.w, self.x, self.z, self.c
        if stage == 0:
            return [(1 - c, place(h, w, x, z, 1 - c))]
        if stage in (1, 4):
            return [(j, place(h, w, j, z, c)) for j in (lax.rem(x + k, 4) for k in range(1, 4))]
        if stage == 2:
            return [(j, on_y(j, x, z, c)) for j in (lax.rem(self.y + k, 4) for k in range(1, 4))]
        return [(j, place(h, w, x, j, c)) for j in (lax.rem(z + k, 8) for k in range(1, 8))]

    def buf(self, stage):
        return (self.pair, *self.slots, self.done)[stage]

    def push(self, stage, i, src):
        for j, dev in self.others(stage):
            pltpu.make_async_remote_copy(src(j), self.buf(stage).at[i], self.ss.at[stage], self.rs.at[stage], device_id=dev, device_id_type=MESH).start()

    def send(self, stage, value):
        i = (self.c, self.x, self.y, self.z, self.x)[stage]
        buf = self.buf(stage)
        if stage == 1:
            for q in range(4):
                self.quarters[q] = value[:, q * 128:q * 128 + 128]
            buf[i] = self.quarters[i]
            self.push(1, i, lambda j: self.quarters.at[j])
        else:
            buf[i] = value
            self.push(stage, i, lambda j: buf.at[i])

    def came(self, stage):
        buf = self.buf(stage)
        part = buf.at[pl.ds(0, buf.shape[0] - 1)]
        pltpu.make_async_copy(part, part, self.rs.at[stage]).wait()

    def total(self, stage):
        self.came(stage)
        buf = self.buf(stage)
        s = buf[0]
        for k in range(1, buf.shape[0]):
            s += buf[k]
        return s

    def result(self, out):
        self.came(4)
        for q in range(4):
            out[:, q * 128:q * 128 + 128] = self.done[q]

    def finish(self):
        for stage in range(5):
            buf = self.buf(stage)
            part = buf.at[pl.ds(0, buf.shape[0] - 1)]
            pltpu.make_async_copy(part, part, self.ss.at[stage]).wait()

def reduction_scratch():
    b = lambda *s: pltpu.VMEM(s, jnp.bfloat16)
    D = pltpu.SemaphoreType.DMA
    return [b(6, 512, 512), b(6, 512, 512), b(6, 256, 512), b(6, 256, 512), b(6, 4, 64, 512), b(6, 64, 512), b(6, 4, 16, 512), b(3, 8, 16, 128), b(3, 8, 16, 128), b(3, 8, 16, 128), D((6, 8)), D((6, 8)), D((6,))]

def tap_scratch():
    D = pltpu.SemaphoreType.DMA
    return [pltpu.VMEM((2, 16, 512), jnp.float32)] + [pltpu.VMEM((n, 16, 128), jnp.float32) for n in (4, 4, 4, 8, 4)] + [D((5,)), D((5,))]

def entry_scratch():
    return [pltpu.SemaphoreType.REGULAR] * 2


def kernel(x_hbm, c_hbm, taps_ref, mix_hbm, o_hbm, gt_out, gm_out, *scratch):
    scratch = list(scratch)
    def take(n):
        got = scratch[:n]
        del scratch[:n]
        return got
    x_ref, c_ref, mix_ref, in_sems = take(4)
    ox, sx, rx, oc, sc, rc, og, sg, rg, tok = take(10)
    pair_sems, sems, loc = take(3)
    xf, act, dg, g, gb, lag, gt = take(7)
    gm, *rest = take(13)
    red = Reduction(gm, gm_out, *rest)
    *bufs, tss, trs = take(8)
    taps = TapSums(bufs, tss, trs)
    plane_sem, all_sem = take(2)
    h, w, x, z, c = coords()

    greet()
    loads = [pltpu.make_async_copy(s, d, in_sems.at[i]) for i, (s, d) in enumerate(((x_hbm, x_ref), (c_hbm, c_ref), (mix_hbm, mix_ref)))]
    for load in loads:
        load.start()
    xf[:, :, 0:PAD] = jnp.zeros((LEVELS, 4, PAD, 128), jnp.float32)
    lag[:, 512:512 + PAD] = jnp.zeros((4, PAD, 128), jnp.float32)
    gt[...] = jnp.zeros((16, 512), jnp.float32)
    meet(plane_sem)
    loads[0].wait()
    tokens_to_tiles(x_ref, sx, ox, c)
    enter(plane_sem, all_sem)
    px = pair_copy(ox, sx, pair_sems, 0)
    px.start()
    spread_one(sx, rx, sems, loc, 0, c)
    loads[1].wait()
    tokens_to_tiles(c_ref, sc, oc, c)
    pc = pair_copy(oc, sc, pair_sems, 1)
    pc.start()
    px.wait_recv()
    spread_one(sx, rx, sems, loc, 3, 1 - c)
    one_arrived(sx, rx, sems, loc, 0)
    pc.wait_recv()
    spread(sc, rc, sems, loc, 1)
    loads[2].wait()
    one_arrived(sx, rx, sems, loc, 3)
    def put_x(i, cg, t):
        xf[0, cg, pl.ds(pl.multiple_of(PAD + i * 64, 32), 64)] = t
    tiles_to_rows(rx, put_x)
    for l in range(LEVELS):
        forward(l, xf, act, dg, taps_ref, mix_ref)

    spread_arrived(sc, rc, sems, loc, 1)
    def put_c(i, cg, t):
        rows = pl.ds(pl.multiple_of(i * 64, 64), 64)
        g[cg, rows] = t
        gb[rows, cg * 128:cg * 128 + 128] = t.astype(jnp.bfloat16)
    tiles_to_rows(rc, put_c)

    for l in reversed(range(LEVELS)):
        gm[l] = mix_grad(l, act, gb).astype(jnp.bfloat16)
        red.halve(l)
        backward(l, xf, dg, g, gb, lag, taps_ref, mix_ref, gt)
        if l == 3:
            red.quarter(5)
            red.quarter(4)
        if l == 2:
            red.quarter(3)
        if l == 1:
            red.quarter(2)
            red.sixteenth(5)
        if l == 0:
            red.sixteenth(4)

    rows_to_tiles(gb, sg, og, c)
    pg = pair_copy(og, sg, pair_sems, 2)
    pg.start()
    red.quarter(0)
    red.quarter(1)
    red.sixteenth(3)
    red.tile(2)
    red.sixteenth(2)
    pg.wait_recv()
    spread(sg, rg, sems, loc, 2, 1, 8)
    taps.send(0, gt[...])
    spread(sg, rg, sems, loc, 2, 8, 16)
    red.sixteenth(0)
    red.sixteenth(1)
    red.untile(2)
    red.tile(1)
    spread(sg, rg, sems, loc, 2, 16, 24)
    spread(sg, rg, sems, loc, 2, 24, 32)
    red.tile(0)
    red.unsixteenth(2)
    red.untile(1)
    spread(sg, rg, sems, loc, 2, 32, 40)
    spread(sg, rg, sems, loc, 2, 40, 48)
    taps.send(1, taps.total(0))
    red.unquarter(2)
    red.untile(0)
    red.unsixteenth(1)
    taps.send(2, taps.total(1))
    spread(sg, rg, sems, loc, 2, 48, 56)
    spread(sg, rg, sems, loc, 2, 56, 64)
    red.unsixteenth(0)
    red.unquarter(1)
    taps.send(3, taps.total(2))
    red.unhalve(2)
    red.unquarter(0)
    spread_arrived(sg, rg, sems, loc, 2)
    tiles_to_tokens(rg, tok)
    tokens = pltpu.make_async_copy(tok, o_hbm, in_sems.at[0])
    tokens.start()
    red.unhalve(1)
    taps.send(4, taps.total(3))
    red.unhalve(0)
    taps.result(gt_out)
    tokens.wait()
    for p in (2, 1, 0):
        red.finish(p)
    taps.finish()
    px.wait_send()
    pc.wait_send()
    pg.wait_send()
    one_sent(sx, rx, sems, 0)
    one_sent(sx, rx, sems, 3)
    spread_sent(sc, rc, sems, 1)
    spread_sent(sg, rg, sems, 2)

def finish(o, gt, gm, o_out, gt_out, gm_out, held_o, held, sems, o_sems):
    ins = [pltpu.make_async_copy(gm.at[l], held.at[l], sems.at[0, l]) for l in range(LEVELS)]
    outs = [pltpu.make_async_copy(held.at[l], gm_out.at[l], sems.at[1, l]) for l in range(LEVELS)]
    for i in range(2):
        rows = pl.ds(i * 256, 256)
        ins.append(pltpu.make_async_copy(o.at[rows], held_o.at[rows], o_sems.at[0, i]))
        outs.append(pltpu.make_async_copy(held_o.at[rows], o_out.at[rows], o_sems.at[1, i]))
    for move in ins:
        move.start()
    for l in range(LEVELS):
        gt_out[l] = gt[2 * l:2 * l + 2]
    for i, move in enumerate(ins):
        move.wait()
        outs[i].start()
    for move in outs:
        move.wait()

def local(inputs, filter_taps, mixing, cotangent):
    f, b = jnp.float32, jnp.bfloat16
    V, S, D = pltpu.VMEM, jax.ShapeDtypeStruct, pltpu.SemaphoreType.DMA
    ANY = pl.BlockSpec(memory_space=pl.ANY)
    loaded = [V((512, 512), b), V((512, 512), b), V((LEVELS, 512, 512), b), D((3,))]
    exchange = ([V((64, 16, 128), b), V((64, 2, 16, 128), b), V((64, 2, 16, 128), b)] * 3) + [V((512, 512), f), D((2, 3)), D((2, 4)), D((4,))]
    levels = [V((LEVELS, 4, PAD + 512, 128), f), V((LEVELS, 512, 512), b), V((LEVELS, 4, 512, 128), f), V((4, 512, 128), f), V((512, 512), b), V((4, 512 + PAD, 128), f), V((16, 512), f)]
    o, gt, gm = pl.pallas_call(
        kernel,
        out_shape=[S((512, 512), f), S((16, 512), f), S((LEVELS, 512, 512), b)],
        in_specs=[ANY, ANY, VM, ANY],
        out_specs=[ANY, VM, ANY],
        scratch_shapes=loaded + exchange + levels + reduction_scratch() + tap_scratch() + entry_scratch(),
        compiler_params=pltpu.CompilerParams(collective_id=1, has_side_effects=True, vmem_limit_bytes=60 << 20),
        cost_estimate=pl.CostEstimate(flops=4831838208, bytes_accessed=10 << 20, transcendentals=1572864),
    )(inputs[0], cotangent[0], filter_taps, mixing)
    o, gt, gm = pl.pallas_call(
        finish,
        out_shape=[S((512, 512), f), S((LEVELS, 2, 512), f), S((LEVELS, 512, 512), b)],
        in_specs=[ANY, VM, ANY],
        out_specs=[ANY, VM, ANY],
        scratch_shapes=[V((512, 512), f), V((LEVELS, 512, 512), b), D((2, LEVELS)), D((2, 2))],
        compiler_params=pltpu.CompilerParams(vmem_limit_bytes=60 << 20),
    )(o, gt, gm)
    return o[None], gt, gm

def solution(mesh):
    halves = P("dp", "seq", None)
    return jax.shard_map(local, mesh=mesh, in_specs=(halves, P(), P(), halves), out_specs=(halves, P(), P()), check_vma=False)
```

```python
import functools, jax, jax.numpy as jnp
from jax import lax
from jax.sharding import PartitionSpec as P
from jax.experimental import pallas as pl
from jax.experimental.pallas import tpu as pltpu
MESH = pl.DeviceIdType.MESH
CHIPS = 64

def coords():
    me = lax.axis_index("seq")
    c = lax.rem(me, 2)
    z = lax.rem(lax.div(me, 2), 8)
    x = lax.rem(lax.div(me, 16), 4)
    w = lax.div(me, 64)
    h = lax.axis_index("dp")
    return h, w, x, z, c

def place(h, w, x, z, c):
    return {"seq": ((w * 4 + x) * 8 + z) * 2 + c, "dp": h}

def on_y(y, x, z, c):
    return place(lax.div(y, 2), lax.rem(y, 2), x, z, c)

def signal(sem, dev):
    pl.semaphore_signal(sem, inc=1, device_id=dev, device_id_type=MESH)

def greet():
    h, w, x, z, c = coords()
    bar = pltpu.get_barrier_semaphore()
    signal(bar, place(h, w, x, z, 1 - c))
    @pl.loop(1, 8)
    def _(k):
        signal(bar, place(h, w, x, lax.rem(z + k, 8), c))
    @pl.loop(1, 4)
    def _(k):
        signal(bar, place(h, w, lax.rem(x + k, 4), z, c))
    y = h * 2 + w
    @pl.loop(1, 4)
    def _(k):
        signal(bar, on_y(lax.rem(y + k, 4), x, z, c))

def meet(plane_sem):
    h, w, x, z, c = coords()
    pl.semaphore_wait(pltpu.get_barrier_semaphore(), 14)
    @pl.loop(1, 4)
    def _(k):
        signal(plane_sem, place(h, w, lax.rem(x + k, 4), z, c))

def enter(plane_sem, all_sem):
    h, w, x, z, c = coords()
    pl.semaphore_wait(plane_sem, 3)
    signal(all_sem, place(h, 1 - w, x, z, c))
    pl.semaphore_wait(all_sem, 1)

def selection(out_of, shape=(256, 256)):
    o = lax.broadcasted_iota(jnp.int32, shape, 0)
    i = lax.broadcasted_iota(jnp.int32, shape, 1)
    return jnp.where(i == out_of(o), 1.0, 0.0).astype(jnp.bfloat16)

def tokens_to_tiles(a_ref, mine, other, c):
    def src(o):
        half, j, cg, n = o // 128, (o // 16) % 8, (o // 4) % 4, o % 4
        return (n * 4 + cg) * 16 + 2 * j + jnp.where(half == 0, c, 1 - c)
    pm = selection(src)
    @pl.loop(0, 8)
    def _(g):
        m = jnp.concatenate([a_ref[pl.ds(pl.multiple_of(n * 128 + g * 16, 16), 16), cg * 128:(cg + 1) * 128] for n in range(4) for cg in range(4)], axis=0)
        t = jnp.dot(pm, m, preferred_element_type=jnp.float32).astype(jnp.bfloat16).reshape(2, 8, 16, 128)
        mine[pl.ds(g * 8, 8), c] = t[0]
        other[pl.ds(g * 8, 8)] = t[1]

def tiles_to_rows(r_ref, put):
    qm = selection(lambda o: ((o // 4) % 16 * 4 + o // 64) * 4 + o % 4)
    @pl.loop(0, 8)
    def _(g):
        m = r_ref[pl.ds(g * 8, 8)].reshape(256, 128)
        t = jnp.dot(qm, m, preferred_element_type=jnp.float32)
        for cg in range(4):
            put(g, cg, t[cg * 64:(cg + 1) * 64])

def rows_to_tiles(g_ref, mine, other, c):
    def src(o):
        half, j, cg, n = o // 128, (o // 16) % 8, (o // 4) % 4, o % 4
        return (cg * 16 + 2 * j + jnp.where(half == 0, c, 1 - c)) * 4 + n
    pm = selection(src)
    @pl.loop(0, 8)
    def _(g):
        m = jnp.concatenate([g_ref[pl.ds(pl.multiple_of(g * 64, 64), 64), cg * 128:(cg + 1) * 128] for cg in range(4)], axis=0)
        t = jnp.dot(pm, m, preferred_element_type=jnp.float32).astype(jnp.bfloat16).reshape(2, 8, 16, 128)
        mine[pl.ds(g * 8, 8), c] = t[0]
        other[pl.ds(g * 8, 8)] = t[1]

def tiles_to_tokens(r_ref, o_ref):
    qm = selection(lambda o: (o % 16 * 4 + (o // 16) % 4) * 4 + o // 64)
    @pl.loop(0, 8)
    def _(g):
        m = r_ref[pl.ds(g * 8, 8)].reshape(256, 128)
        t = jnp.dot(qm, m, preferred_element_type=jnp.float32)
        for n in range(4):
            for cg in range(4):
                o_ref[pl.ds(pl.multiple_of(n * 128 + g * 16, 16), 16), cg * 128:(cg + 1) * 128] = t[(n * 4 + cg) * 16:(n * 4 + cg + 1) * 16]

def pair_copy(other, s_ref, sems, k):
    h, w, x, z, c = coords()
    return pltpu.make_async_remote_copy(other, s_ref.at[:, c], sems.at[0, k], sems.at[1, k], device_id=place(h, w, x, z, 1 - c), device_id_type=MESH)

def spread(s_ref, r_ref, sems, loc, k, begin=1, end=64):
    h, w, x, z, c = coords()
    j = (w * 4 + x) * 8 + z
    if begin == 1:
        pltpu.make_async_copy(s_ref.at[j], r_ref.at[j], loc.at[k]).start()
    @pl.loop(begin, end)
    def _(t):
        b = lax.rem(t, 8)
        a = lax.div(t, 8)
        dz = jnp.where(lax.rem(b, 2) == 1, lax.div(b + 1, 2), 8 - lax.div(b, 2))
        z2 = lax.rem(z + dz, 8)
        x2 = lax.rem(x + lax.rem(a, 4), 4)
        w2 = lax.rem(w + lax.div(a, 4), 2)
        pltpu.make_async_remote_copy(s_ref.at[(w2 * 4 + x2) * 8 + z2], r_ref.at[j], sems.at[0, k], sems.at[1, k], device_id=place(h, w2, x2, z2, c), device_id_type=MESH).start()

def spread_one(s_ref, r_ref, sems, loc, k, core):
    h, w, x, z, c = coords()
    j = (w * 4 + x) * 8 + z
    pltpu.make_async_copy(s_ref.at[j, core], r_ref.at[j, core], loc.at[k]).start()
    @pl.loop(1, 64)
    def _(t):
        b = lax.rem(t, 8)
        a = lax.div(t, 8)
        dz = jnp.where(lax.rem(b, 2) == 1, lax.div(b + 1, 2), 8 - lax.div(b, 2))
        z2 = lax.rem(z + dz, 8)
        x2 = lax.rem(x + lax.rem(a, 4), 4)
        w2 = lax.rem(w + lax.div(a, 4), 2)
        pltpu.make_async_remote_copy(s_ref.at[(w2 * 4 + x2) * 8 + z2, core], r_ref.at[j, core], sems.at[0, k], sems.at[1, k], device_id=place(h, w2, x2, z2, c), device_id_type=MESH).start()

def one_arrived(s_ref, r_ref, sems, loc, k):
    h, w, x, z, c = coords()
    j = (w * 4 + x) * 8 + z
    pltpu.make_async_copy(s_ref.at[j, 0], r_ref.at[j, 0], loc.at[k]).wait()
    some = pl.ds(0, 63)
    pltpu.make_async_copy(s_ref.at[some, 0], r_ref.at[some, 0], sems.at[1, k]).wait()

def one_sent(s_ref, r_ref, sems, k):
    some = pl.ds(0, 63)
    pltpu.make_async_copy(s_ref.at[some, 0], r_ref.at[some, 0], sems.at[0, k]).wait()

def spread_arrived(s_ref, r_ref, sems, loc, k, begin=1, end=64):
    h, w, x, z, c = coords()
    j = (w * 4 + x) * 8 + z
    if begin == 1:
        pltpu.make_async_copy(s_ref.at[j], r_ref.at[j], loc.at[k]).wait()
    some = pl.ds(0, end - begin)
    pltpu.make_async_copy(s_ref.at[some], r_ref.at[some], sems.at[1, k]).wait()

def spread_sent(s_ref, r_ref, sems, k, begin=1, end=64):
    some = pl.ds(0, end - begin)
    pltpu.make_async_copy(s_ref.at[some], r_ref.at[some], sems.at[0, k]).wait()

LEVELS = 6
K0 = 0.7978845608028654
K1C = K0 * 0.044715
PAD = 32
TILE = 128

def forward(l, xf, act, dg, taps_ref, mix_ref):
    d = 1 << l
    for rt in range(512 // TILE):
        r0 = rt * TILE
        for cg in range(4):
            lanes = slice(cg * 128, cg * 128 + 128)
            cur = xf[l, cg, PAD + r0:PAD + r0 + TILE]
            lag = xf[l, cg, PAD + r0 - d:PAD + r0 - d + TILE]
            p = taps_ref[l, 0:1, lanes] * cur + taps_ref[l, 1:2, lanes] * lag
            p2 = p * p
            t = jnp.tanh(p * (K0 + K1C * p2))
            half = 0.5 + 0.5 * t
            act[l, r0:r0 + TILE, lanes] = (p * half).astype(jnp.bfloat16)
            dg[l, cg, r0:r0 + TILE] = half + (half * (1.0 - half) * p) * (2 * K0 + 6 * K1C * p2)
        if l + 1 < LEVELS:
            m = jnp.dot(act[l, r0:r0 + TILE, :], mix_ref[l], preferred_element_type=jnp.float32)
            for cg in range(4):
                nxt = xf[l, cg, PAD + r0:PAD + r0 + TILE] + m[:, cg * 128:cg * 128 + 128]
                xf[l + 1, cg, PAD + r0:PAD + r0 + TILE] = nxt.astype(jnp.bfloat16).astype(jnp.float32)

def backward(l, xf, dg, g, gb, lag, taps_ref, mix_ref, gtaps):
    d = 1 << l
    sums = [[jnp.zeros((8, 128), jnp.float32) for _ in range(2)] for _ in range(4)]
    for rt in reversed(range(512 // TILE)):
        r0 = rt * TILE
        ga = lax.dot_general(gb[r0:r0 + TILE, :], mix_ref[l], (((1,), (1,)), ((), ())), preferred_element_type=jnp.float32)
        for cg in range(4):
            lanes = slice(cg * 128, cg * 128 + 128)
            gp = ga[:, lanes] * dg[l, cg, r0:r0 + TILE]
            cur = xf[l, cg, PAD + r0:PAD + r0 + TILE]
            old = xf[l, cg, PAD + r0 - d:PAD + r0 - d + TILE]
            sums[cg][0] += jnp.sum((gp * cur).reshape(TILE // 8, 8, 128), axis=0)
            sums[cg][1] += jnp.sum((gp * old).reshape(TILE // 8, 8, 128), axis=0)
            lag[cg, r0:r0 + TILE] = (taps_ref[l, 1:2, lanes] * gp).astype(jnp.bfloat16).astype(jnp.float32)
            new = g[cg, r0:r0 + TILE] + taps_ref[l, 0:1, lanes] * gp + lag[cg, r0 + d:r0 + d + TILE]
            g[cg, r0:r0 + TILE] = new
            gb[r0:r0 + TILE, lanes] = new.astype(jnp.bfloat16)
    for cg in range(4):
        for k in range(2):
            gtaps[2 * l + k:2 * l + k + 1, cg * 128:cg * 128 + 128] = jnp.sum(sums[cg][k], axis=0, keepdims=True)

def mix_grad(l, act, gb):
    return lax.dot_general(act[l], gb[...], (((0,), (0,)), ((), ())), preferred_element_type=jnp.float32)


VM = pl.BlockSpec(memory_space=pltpu.VMEM)

class Reduction:
    def __init__(self, gm, final, out, c0, hh, r1, qq, r2, e8, r3, f8, ss, rs, ls):
        self.__dict__.update(gm=gm, final=final, out=out, ls=ls, c0=c0, hh=hh, r1=r1, qq=qq, r2=r2, e8=e8, r3=r3, f8=f8, ss=ss, rs=rs)
        self.h, self.w, self.x, self.z, self.c = h, w, x, z, c = coords()
        self.y = h * 2 + w
        others = lambda i, n: [lax.rem(i + k, n) for k in sorted(range(1, n), key=lambda k: -min(k, n - k))]
        self.on_axis = {1: [(j, place(h, w, j, z, c)) for j in others(x, 4)], 0: [(j, on_y(j, x, z, c)) for j in others(self.y, 4)]}
        self.on_z = [(j, place(h, w, x, j, c)) for j in others(z, 8)]

    def first(self, l):
        return self.x if l % 2 else self.y

    def second(self, l):
        return self.y if l % 2 else self.x

    def copy(self, src, dst, l, stage, dev):
        return pltpu.make_async_remote_copy(src, dst, self.ss.at[l, stage], self.rs.at[l, stage], device_id=dev, device_id_type=MESH)

    def other_core(self):
        return place(self.h, self.w, self.x, self.z, 1 - self.c)

    def rows(self, l):
        r256 = self.c * 256
        r64 = r256 + self.first(l) * 64
        return pl.multiple_of(r256, 256), pl.multiple_of(r64, 64), pl.multiple_of(r64 + self.second(l) * 16, 16)

    def took(self, ref, l, stage):
        pltpu.make_async_copy(ref, ref, self.rs.at[l, stage]).wait()

    def gave(self, ref, l, stage):
        pltpu.make_async_copy(ref, ref, self.ss.at[l, stage]).wait()

    def halve(self, l):
        far = pl.multiple_of((1 - self.c) * 256, 256)
        self.copy(self.gm.at[l, pl.ds(far, 256)], self.c0.at[l], l, 0, self.other_core()).start()

    def quarter(self, l):
        self.took(self.c0.at[l], l, 0)
        near = self.rows(l)[0]
        self.hh[l] = (self.gm[l, pl.ds(near, 256)].astype(jnp.float32) + self.c0[l].astype(jnp.float32)).astype(jnp.bfloat16)
        i = self.first(l)
        for j, dev in self.on_axis[l % 2]:
            self.copy(self.hh.at[l, pl.ds(pl.multiple_of(j * 64, 64), 64)], self.r1.at[l, i], l, 1, dev).start()

    def sixteenth(self, l):
        self.took(self.r1.at[l, pl.ds(0, 3)], l, 1)
        i = self.first(l)
        s = self.hh[l, pl.ds(pl.multiple_of(i * 64, 64), 64)].astype(jnp.float32)
        for k in range(1, 4):
            s += self.r1[l, lax.rem(i + k, 4)].astype(jnp.float32)
        self.qq[l] = s.astype(jnp.bfloat16)
        i2 = self.second(l)
        for j, dev in self.on_axis[1 - l % 2]:
            self.copy(self.qq.at[l, pl.ds(pl.multiple_of(j * 16, 16), 16)], self.r2.at[l, i2], l, 2, dev).start()

    def tile(self, p):
        z = self.z
        for l in (2 * p, 2 * p + 1):
            self.took(self.r2.at[l, pl.ds(0, 3)], l, 2)
            i2 = self.second(l)
            s = self.qq[l, pl.ds(pl.multiple_of(i2 * 16, 16), 16)].astype(jnp.float32)
            for k in range(1, 4):
                s += self.r2[l, lax.rem(i2 + k, 4)].astype(jnp.float32)
            for cg in range(4):
                self.e8[p, l % 2 * 4 + cg] = s[:, cg * 128:cg * 128 + 128].astype(jnp.bfloat16)
        for j, dev in self.on_z:
            self.copy(self.e8.at[p, j], self.r3.at[p, z], 2 * p, 3, dev).start()

    def untile(self, p):
        z = self.z
        self.took(self.r3.at[p, pl.ds(0, 7)], 2 * p, 3)
        s = self.e8[p, z].astype(jnp.float32)
        for k in range(1, 8):
            s += self.r3[p, lax.rem(z + k, 8)].astype(jnp.float32)
        self.f8[p, z] = s.astype(jnp.bfloat16)
        for j, dev in self.on_z:
            self.copy(self.f8.at[p, z], self.f8.at[p, z], 2 * p, 4, dev).start()

    def unsixteenth(self, p):
        self.took(self.f8.at[p, pl.ds(0, 7)], 2 * p, 4)
        for l in (2 * p, 2 * p + 1):
            r16 = self.rows(l)[2]
            for cg in range(4):
                self.out[l, pl.ds(r16, 16), cg * 128:cg * 128 + 128] = self.f8[p, l % 2 * 4 + cg]
            mine = self.out.at[l, pl.ds(r16, 16)]
            for j, dev in self.on_axis[1 - l % 2]:
                self.copy(mine, mine, l, 5, dev).start()

    def unquarter(self, p):
        for l in (2 * p, 2 * p + 1):
            self.took(self.out.at[l, pl.ds(0, 48)], l, 5)
            mine = self.out.at[l, pl.ds(self.rows(l)[1], 64)]
            for j, dev in self.on_axis[l % 2]:
                self.copy(mine, mine, l, 6, dev).start()

    def unhalve(self, p):
        for l in (2 * p, 2 * p + 1):
            self.took(self.out.at[l, pl.ds(0, 192)], l, 6)
            mine = self.out.at[l, pl.ds(self.rows(l)[0], 256)]
            there = self.final.at[l, pl.ds(self.rows(l)[0], 256)]
            self.copy(mine, there, l, 7, self.other_core()).start()
            pltpu.make_async_copy(mine, there, self.ls.at[l]).start()

    def settle(self, p):
        for l in (2 * p, 2 * p + 1):
            self.gave(self.c0.at[l], l, 0)
            self.gave(self.r1.at[l, pl.ds(0, 3)], l, 1)
            self.gave(self.r2.at[l, pl.ds(0, 3)], l, 2)
            self.gave(self.out.at[l, pl.ds(0, 48)], l, 5)
            self.gave(self.out.at[l, pl.ds(0, 192)], l, 6)
        self.gave(self.r3.at[p, pl.ds(0, 7)], 2 * p, 3)
        self.gave(self.f8.at[p, pl.ds(0, 7)], 2 * p, 4)

    def finish(self, p):
        for l in (2 * p, 2 * p + 1):
            half = self.final.at[l, pl.ds(0, 256)]
            pltpu.make_async_copy(half, half, self.ls.at[l]).wait()
            self.gave(self.out.at[l, pl.ds(0, 256)], l, 7)
            self.took(half, l, 7)

class TapSums:
    def __init__(self, bufs, ss, rs):
        self.pair, self.quarters, *self.slots, self.done = bufs
        self.ss, self.rs = ss, rs
        self.h, self.w, self.x, self.z, self.c = coords()
        self.y = self.h * 2 + self.w

    def others(self, stage):
        h, w, x, z, c = self.h, self.w, self.x, self.z, self.c
        if stage == 0:
            return [(1 - c, place(h, w, x, z, 1 - c))]
        if stage in (1, 4):
            return [(j, place(h, w, j, z, c)) for j in (lax.rem(x + k, 4) for k in range(1, 4))]
        if stage == 2:
            return [(j, on_y(j, x, z, c)) for j in (lax.rem(self.y + k, 4) for k in range(1, 4))]
        return [(j, place(h, w, x, j, c)) for j in (lax.rem(z + k, 8) for k in range(1, 8))]

    def buf(self, stage):
        return (self.pair, *self.slots, self.done)[stage]

    def push(self, stage, i, src):
        for j, dev in self.others(stage):
            pltpu.make_async_remote_copy(src(j), self.buf(stage).at[i], self.ss.at[stage], self.rs.at[stage], device_id=dev, device_id_type=MESH).start()

    def send(self, stage, value):
        i = (self.c, self.x, self.y, self.z, self.x)[stage]
        buf = self.buf(stage)
        if stage == 1:
            for q in range(4):
                self.quarters[q] = value[:, q * 128:q * 128 + 128]
            buf[i] = self.quarters[i]
            self.push(1, i, lambda j: self.quarters.at[j])
        else:
            buf[i] = value
            self.push(stage, i, lambda j: buf.at[i])

    def came(self, stage):
        buf = self.buf(stage)
        part = buf.at[pl.ds(0, buf.shape[0] - 1)]
        pltpu.make_async_copy(part, part, self.rs.at[stage]).wait()

    def total(self, stage):
        self.came(stage)
        buf = self.buf(stage)
        s = buf[0]
        for k in range(1, buf.shape[0]):
            s += buf[k]
        return s

    def result(self, out):
        self.came(4)
        for q in range(4):
            out[:, q * 128:q * 128 + 128] = self.done[q]

    def finish(self):
        for stage in range(5):
            buf = self.buf(stage)
            part = buf.at[pl.ds(0, buf.shape[0] - 1)]
            pltpu.make_async_copy(part, part, self.ss.at[stage]).wait()

def reduction_scratch():
    b = lambda *s: pltpu.VMEM(s, jnp.bfloat16)
    D = pltpu.SemaphoreType.DMA
    return [b(6, 512, 512), b(6, 512, 512), b(6, 256, 512), b(6, 256, 512), b(6, 4, 64, 512), b(6, 64, 512), b(6, 4, 16, 512), b(3, 8, 16, 128), b(3, 8, 16, 128), b(3, 8, 16, 128), D((6, 8)), D((6, 8)), D((6,))]

def tap_scratch():
    D = pltpu.SemaphoreType.DMA
    return [pltpu.VMEM((2, 16, 512), jnp.float32)] + [pltpu.VMEM((n, 16, 128), jnp.float32) for n in (4, 4, 4, 8, 4)] + [D((5,)), D((5,))]

def entry_scratch():
    return [pltpu.SemaphoreType.REGULAR] * 2


def kernel(x_hbm, c_hbm, taps_ref, mix_hbm, o_hbm, gt_out, gm_out, *scratch):
    scratch = list(scratch)
    def take(n):
        got = scratch[:n]
        del scratch[:n]
        return got
    x_ref, c_ref, mix_ref, in_sems = take(4)
    ox, sx, rx, oc, sc, rc, og, sg, rg, tok = take(10)
    pair_sems, sems, loc = take(3)
    xf, act, dg, g, gb, lag, gt = take(7)
    gm, *rest = take(13)
    red = Reduction(gm, gm_out, *rest)
    *bufs, tss, trs = take(8)
    taps = TapSums(bufs, tss, trs)
    plane_sem, all_sem = take(2)
    h, w, x, z, c = coords()

    greet()
    loads = [pltpu.make_async_copy(s, d, in_sems.at[i]) for i, (s, d) in enumerate(((x_hbm, x_ref), (c_hbm, c_ref), (mix_hbm, mix_ref)))]
    for load in loads:
        load.start()
    xf[:, :, 0:PAD] = jnp.zeros((LEVELS, 4, PAD, 128), jnp.float32)
    lag[:, 512:512 + PAD] = jnp.zeros((4, PAD, 128), jnp.float32)
    gt[...] = jnp.zeros((16, 512), jnp.float32)
    meet(plane_sem)
    loads[0].wait()
    tokens_to_tiles(x_ref, sx, ox, c)
    enter(plane_sem, all_sem)
    px = pair_copy(ox, sx, pair_sems, 0)
    px.start()
    spread_one(sx, rx, sems, loc, 0, c)
    loads[1].wait()
    tokens_to_tiles(c_ref, sc, oc, c)
    pc = pair_copy(oc, sc, pair_sems, 1)
    pc.start()
    px.wait_recv()
    spread_one(sx, rx, sems, loc, 3, 1 - c)
    one_arrived(sx, rx, sems, loc, 0)
    pc.wait_recv()
    spread(sc, rc, sems, loc, 1)
    loads[2].wait()
    one_arrived(sx, rx, sems, loc, 3)
    def put_x(i, cg, t):
        xf[0, cg, pl.ds(pl.multiple_of(PAD + i * 64, 32), 64)] = t
    tiles_to_rows(rx, put_x)
    for l in range(LEVELS):
        forward(l, xf, act, dg, taps_ref, mix_ref)

    spread_arrived(sc, rc, sems, loc, 1)
    def put_c(i, cg, t):
        rows = pl.ds(pl.multiple_of(i * 64, 64), 64)
        g[cg, rows] = t
        gb[rows, cg * 128:cg * 128 + 128] = t.astype(jnp.bfloat16)
    tiles_to_rows(rc, put_c)

    for l in reversed(range(LEVELS)):
        gm[l] = mix_grad(l, act, gb).astype(jnp.bfloat16)
        red.halve(l)
        backward(l, xf, dg, g, gb, lag, taps_ref, mix_ref, gt)
        if l == 3:
            red.quarter(5)
            red.quarter(4)
        if l == 2:
            red.quarter(3)
        if l == 1:
            red.quarter(2)

    rows_to_tiles(gb, sg, og, c)
    pg = pair_copy(og, sg, pair_sems, 2)
    pg.start()
    red.sixteenth(5)
    red.sixteenth(4)
    red.sixteenth(3)
    red.quarter(0)
    red.sixteenth(2)
    red.quarter(1)
    taps.send(0, gt[...])
    red.tile(2)
    pg.wait_recv()
    spread(sg, rg, sems, loc, 2, 1, 8)
    red.tile(1)
    spread(sg, rg, sems, loc, 2, 8, 16)
    red.sixteenth(0)
    taps.send(1, taps.total(0))
    red.sixteenth(1)
    red.untile(2)
    spread(sg, rg, sems, loc, 2, 16, 24)
    red.untile(1)
    red.tile(0)
    spread(sg, rg, sems, loc, 2, 24, 32)
    red.unsixteenth(2)
    spread(sg, rg, sems, loc, 2, 32, 40)
    spread(sg, rg, sems, loc, 2, 40, 48)
    red.unsixteenth(1)
    red.unquarter(2)
    red.untile(0)
    spread(sg, rg, sems, loc, 2, 48, 56)
    taps.send(2, taps.total(1))
    spread(sg, rg, sems, loc, 2, 56, 64)
    red.unsixteenth(0)
    red.unquarter(1)
    taps.send(3, taps.total(2))
    red.unhalve(2)
    red.unquarter(0)
    red.unhalve(1)
    spread_arrived(sg, rg, sems, loc, 2)
    tiles_to_tokens(rg, tok)
    tokens = pltpu.make_async_copy(tok, o_hbm, in_sems.at[0])
    tokens.start()
    taps.send(4, taps.total(3))
    red.unhalve(0)
    taps.result(gt_out)
    taps.finish()
    px.wait_send()
    pc.wait_send()
    pg.wait_send()
    one_sent(sx, rx, sems, 0)
    one_sent(sx, rx, sems, 3)
    spread_sent(sc, rc, sems, 1)
    spread_sent(sg, rg, sems, 2)
    for p in (2, 1, 0):
        red.settle(p)
    tokens.wait()
    for p in (2, 1, 0):
        red.finish(p)

def finish(o, gt, gm, o_out, gt_out, gm_out, held_o, held, sems, o_sems):
    ins = [pltpu.make_async_copy(gm.at[l], held.at[l], sems.at[0, l]) for l in range(LEVELS)]
    outs = [pltpu.make_async_copy(held.at[l], gm_out.at[l], sems.at[1, l]) for l in range(LEVELS)]
    for i in range(2):
        rows = pl.ds(i * 256, 256)
        ins.append(pltpu.make_async_copy(o.at[rows], held_o.at[rows], o_sems.at[0, i]))
        outs.append(pltpu.make_async_copy(held_o.at[rows], o_out.at[rows], o_sems.at[1, i]))
    for move in ins:
        move.start()
    for l in range(LEVELS):
        gt_out[l] = gt[2 * l:2 * l + 2]
    for i, move in enumerate(ins):
        move.wait()
        outs[i].start()
    for move in outs:
        move.wait()

def local(inputs, filter_taps, mixing, cotangent):
    f, b = jnp.float32, jnp.bfloat16
    V, S, D = pltpu.VMEM, jax.ShapeDtypeStruct, pltpu.SemaphoreType.DMA
    ANY = pl.BlockSpec(memory_space=pl.ANY)
    loaded = [V((512, 512), b), V((512, 512), b), V((LEVELS, 512, 512), b), D((3,))]
    exchange = ([V((64, 16, 128), b), V((64, 2, 16, 128), b), V((64, 2, 16, 128), b)] * 3) + [V((512, 512), f), D((2, 3)), D((2, 4)), D((4,))]
    levels = [V((LEVELS, 4, PAD + 512, 128), f), V((LEVELS, 512, 512), b), V((LEVELS, 4, 512, 128), f), V((4, 512, 128), f), V((512, 512), b), V((4, 512 + PAD, 128), f), V((16, 512), f)]
    o, gt, gm = pl.pallas_call(
        kernel,
        out_shape=[S((512, 512), f), S((16, 512), f), S((LEVELS, 512, 512), b)],
        in_specs=[ANY, ANY, VM, ANY],
        out_specs=[ANY, VM, ANY],
        scratch_shapes=loaded + exchange + levels + reduction_scratch() + tap_scratch() + entry_scratch(),
        compiler_params=pltpu.CompilerParams(collective_id=1, has_side_effects=True, vmem_limit_bytes=60 << 20),
        cost_estimate=pl.CostEstimate(flops=4831838208, bytes_accessed=10 << 20, transcendentals=1572864),
    )(inputs[0], cotangent[0], filter_taps, mixing)
    o, gt, gm = pl.pallas_call(
        finish,
        out_shape=[S((512, 512), f), S((LEVELS, 2, 512), f), S((LEVELS, 512, 512), b)],
        in_specs=[ANY, VM, ANY],
        out_specs=[ANY, VM, ANY],
        scratch_shapes=[V((512, 512), f), V((LEVELS, 512, 512), b), D((2, LEVELS)), D((2, 2))],
        compiler_params=pltpu.CompilerParams(vmem_limit_bytes=60 << 20),
    )(o, gt, gm)
    return o[None], gt, gm

def solution(mesh):
    halves = P("dp", "seq", None)
    return jax.shard_map(local, mesh=mesh, in_specs=(halves, P(), P(), halves), out_specs=(halves, P(), P()), check_vma=False)
```

```python
import functools, jax, jax.numpy as jnp
from jax import lax
from jax.sharding import PartitionSpec as P
from jax.experimental import pallas as pl
from jax.experimental.pallas import tpu as pltpu
MESH = pl.DeviceIdType.MESH
CHIPS = 64

def coords():
    me = lax.axis_index("seq")
    c = lax.rem(me, 2)
    z = lax.rem(lax.div(me, 2), 8)
    x = lax.rem(lax.div(me, 16), 4)
    w = lax.div(me, 64)
    h = lax.axis_index("dp")
    return h, w, x, z, c

def place(h, w, x, z, c):
    return {"seq": ((w * 4 + x) * 8 + z) * 2 + c, "dp": h}

def on_y(y, x, z, c):
    return place(lax.div(y, 2), lax.rem(y, 2), x, z, c)

def signal(sem, dev):
    pl.semaphore_signal(sem, inc=1, device_id=dev, device_id_type=MESH)

def greet():
    h, w, x, z, c = coords()
    bar = pltpu.get_barrier_semaphore()
    signal(bar, place(h, w, x, z, 1 - c))
    @pl.loop(1, 8)
    def _(k):
        signal(bar, place(h, w, x, lax.rem(z + k, 8), c))
    @pl.loop(1, 4)
    def _(k):
        signal(bar, place(h, w, lax.rem(x + k, 4), z, c))
    y = h * 2 + w
    @pl.loop(1, 4)
    def _(k):
        signal(bar, on_y(lax.rem(y + k, 4), x, z, c))

def meet(plane_sem):
    h, w, x, z, c = coords()
    pl.semaphore_wait(pltpu.get_barrier_semaphore(), 14)
    @pl.loop(1, 4)
    def _(k):
        signal(plane_sem, place(h, w, lax.rem(x + k, 4), z, c))

def enter(plane_sem, all_sem):
    h, w, x, z, c = coords()
    pl.semaphore_wait(plane_sem, 3)
    signal(all_sem, place(h, 1 - w, x, z, c))
    pl.semaphore_wait(all_sem, 1)

def selection(out_of, shape=(256, 256)):
    o = lax.broadcasted_iota(jnp.int32, shape, 0)
    i = lax.broadcasted_iota(jnp.int32, shape, 1)
    return jnp.where(i == out_of(o), 1.0, 0.0).astype(jnp.bfloat16)

def tokens_to_tiles(a_ref, mine, other, c):
    def src(o):
        half, j, cg, n = o // 128, (o // 16) % 8, (o // 4) % 4, o % 4
        return (n * 4 + cg) * 16 + 2 * j + jnp.where(half == 0, c, 1 - c)
    pm = selection(src)
    @pl.loop(0, 8)
    def _(g):
        m = jnp.concatenate([a_ref[pl.ds(pl.multiple_of(n * 128 + g * 16, 16), 16), cg * 128:(cg + 1) * 128] for n in range(4) for cg in range(4)], axis=0)
        t = jnp.dot(pm, m, preferred_element_type=jnp.float32).astype(jnp.bfloat16).reshape(2, 8, 16, 128)
        mine[pl.ds(g * 8, 8), c] = t[0]
        other[pl.ds(g * 8, 8)] = t[1]

def tiles_to_rows(r_ref, put):
    qm = selection(lambda o: ((o // 4) % 16 * 4 + o // 64) * 4 + o % 4)
    @pl.loop(0, 8)
    def _(g):
        m = r_ref[pl.ds(g * 8, 8)].reshape(256, 128)
        t = jnp.dot(qm, m, preferred_element_type=jnp.float32)
        for cg in range(4):
            put(g, cg, t[cg * 64:(cg + 1) * 64])

def rows_to_tiles(g_ref, mine, other, c):
    def src(o):
        half, j, cg, n = o // 128, (o // 16) % 8, (o // 4) % 4, o % 4
        return (cg * 16 + 2 * j + jnp.where(half == 0, c, 1 - c)) * 4 + n
    pm = selection(src)
    @pl.loop(0, 8)
    def _(g):
        m = jnp.concatenate([g_ref[pl.ds(pl.multiple_of(g * 64, 64), 64), cg * 128:(cg + 1) * 128] for cg in range(4)], axis=0)
        t = jnp.dot(pm, m, preferred_element_type=jnp.float32).astype(jnp.bfloat16).reshape(2, 8, 16, 128)
        mine[pl.ds(g * 8, 8), c] = t[0]
        other[pl.ds(g * 8, 8)] = t[1]

def tiles_to_tokens(r_ref, o_ref):
    qm = selection(lambda o: (o % 16 * 4 + (o // 16) % 4) * 4 + o // 64)
    @pl.loop(0, 8)
    def _(g):
        m = r_ref[pl.ds(g * 8, 8)].reshape(256, 128)
        t = jnp.dot(qm, m, preferred_element_type=jnp.float32)
        for n in range(4):
            for cg in range(4):
                o_ref[pl.ds(pl.multiple_of(n * 128 + g * 16, 16), 16), cg * 128:(cg + 1) * 128] = t[(n * 4 + cg) * 16:(n * 4 + cg + 1) * 16]

def pair_copy(other, s_ref, sems, k):
    h, w, x, z, c = coords()
    return pltpu.make_async_remote_copy(other, s_ref.at[:, c], sems.at[0, k], sems.at[1, k], device_id=place(h, w, x, z, 1 - c), device_id_type=MESH)

def spread(s_ref, r_ref, sems, loc, k, begin=1, end=64):
    h, w, x, z, c = coords()
    j = (w * 4 + x) * 8 + z
    if begin == 1:
        pltpu.make_async_copy(s_ref.at[j], r_ref.at[j], loc.at[k]).start()
    @pl.loop(begin, end)
    def _(t):
        b = lax.rem(t, 8)
        a = lax.div(t, 8)
        dz = jnp.where(lax.rem(b, 2) == 1, lax.div(b + 1, 2), 8 - lax.div(b, 2))
        z2 = lax.rem(z + dz, 8)
        x2 = lax.rem(x + lax.rem(a, 4), 4)
        w2 = lax.rem(w + lax.div(a, 4), 2)
        pltpu.make_async_remote_copy(s_ref.at[(w2 * 4 + x2) * 8 + z2], r_ref.at[j], sems.at[0, k], sems.at[1, k], device_id=place(h, w2, x2, z2, c), device_id_type=MESH).start()

def spread_one(s_ref, r_ref, sems, loc, k, core):
    h, w, x, z, c = coords()
    j = (w * 4 + x) * 8 + z
    pltpu.make_async_copy(s_ref.at[j, core], r_ref.at[j, core], loc.at[k]).start()
    @pl.loop(1, 64)
    def _(t):
        b = lax.rem(t, 8)
        a = lax.div(t, 8)
        dz = jnp.where(lax.rem(b, 2) == 1, lax.div(b + 1, 2), 8 - lax.div(b, 2))
        z2 = lax.rem(z + dz, 8)
        x2 = lax.rem(x + lax.rem(a, 4), 4)
        w2 = lax.rem(w + lax.div(a, 4), 2)
        pltpu.make_async_remote_copy(s_ref.at[(w2 * 4 + x2) * 8 + z2, core], r_ref.at[j, core], sems.at[0, k], sems.at[1, k], device_id=place(h, w2, x2, z2, c), device_id_type=MESH).start()

def one_arrived(s_ref, r_ref, sems, loc, k):
    h, w, x, z, c = coords()
    j = (w * 4 + x) * 8 + z
    pltpu.make_async_copy(s_ref.at[j, 0], r_ref.at[j, 0], loc.at[k]).wait()
    some = pl.ds(0, 63)
    pltpu.make_async_copy(s_ref.at[some, 0], r_ref.at[some, 0], sems.at[1, k]).wait()

def one_sent(s_ref, r_ref, sems, k):
    some = pl.ds(0, 63)
    pltpu.make_async_copy(s_ref.at[some, 0], r_ref.at[some, 0], sems.at[0, k]).wait()

def spread_arrived(s_ref, r_ref, sems, loc, k, begin=1, end=64):
    h, w, x, z, c = coords()
    j = (w * 4 + x) * 8 + z
    if begin == 1:
        pltpu.make_async_copy(s_ref.at[j], r_ref.at[j], loc.at[k]).wait()
    some = pl.ds(0, end - begin)
    pltpu.make_async_copy(s_ref.at[some], r_ref.at[some], sems.at[1, k]).wait()

def spread_sent(s_ref, r_ref, sems, k, begin=1, end=64):
    some = pl.ds(0, end - begin)
    pltpu.make_async_copy(s_ref.at[some], r_ref.at[some], sems.at[0, k]).wait()

LEVELS = 6
K0 = 0.7978845608028654
K1C = K0 * 0.044715
PAD = 32
TILE = 128

def forward(l, xf, act, dg, taps_ref, mix_ref):
    d = 1 << l
    for rt in range(512 // TILE):
        r0 = rt * TILE
        for cg in range(4):
            lanes = slice(cg * 128, cg * 128 + 128)
            cur = xf[l, cg, PAD + r0:PAD + r0 + TILE]
            lag = xf[l, cg, PAD + r0 - d:PAD + r0 - d + TILE]
            p = taps_ref[l, 0:1, lanes] * cur + taps_ref[l, 1:2, lanes] * lag
            p2 = p * p
            t = jnp.tanh(p * (K0 + K1C * p2))
            half = 0.5 + 0.5 * t
            act[l, r0:r0 + TILE, lanes] = (p * half).astype(jnp.bfloat16)
            dg[l, cg, r0:r0 + TILE] = half + (half * (1.0 - half) * p) * (2 * K0 + 6 * K1C * p2)
        if l + 1 < LEVELS:
            m = jnp.dot(act[l, r0:r0 + TILE, :], mix_ref[l], preferred_element_type=jnp.float32)
            for cg in range(4):
                nxt = xf[l, cg, PAD + r0:PAD + r0 + TILE] + m[:, cg * 128:cg * 128 + 128]
                xf[l + 1, cg, PAD + r0:PAD + r0 + TILE] = nxt.astype(jnp.bfloat16).astype(jnp.float32)

def backward(l, xf, dg, g, gb, lag, taps_ref, mix_ref, gtaps):
    d = 1 << l
    sums = [[jnp.zeros((8, 128), jnp.float32) for _ in range(2)] for _ in range(4)]
    for rt in reversed(range(512 // TILE)):
        r0 = rt * TILE
        ga = lax.dot_general(gb[r0:r0 + TILE, :], mix_ref[l], (((1,), (1,)), ((), ())), preferred_element_type=jnp.float32)
        for cg in range(4):
            lanes = slice(cg * 128, cg * 128 + 128)
            gp = ga[:, lanes] * dg[l, cg, r0:r0 + TILE]
            cur = xf[l, cg, PAD + r0:PAD + r0 + TILE]
            old = xf[l, cg, PAD + r0 - d:PAD + r0 - d + TILE]
            sums[cg][0] += jnp.sum((gp * cur).reshape(TILE // 8, 8, 128), axis=0)
            sums[cg][1] += jnp.sum((gp * old).reshape(TILE // 8, 8, 128), axis=0)
            lag[cg, r0:r0 + TILE] = (taps_ref[l, 1:2, lanes] * gp).astype(jnp.bfloat16).astype(jnp.float32)
            new = g[cg, r0:r0 + TILE] + taps_ref[l, 0:1, lanes] * gp + lag[cg, r0 + d:r0 + d + TILE]
            g[cg, r0:r0 + TILE] = new
            gb[r0:r0 + TILE, lanes] = new.astype(jnp.bfloat16)
    for cg in range(4):
        for k in range(2):
            gtaps[2 * l + k:2 * l + k + 1, cg * 128:cg * 128 + 128] = jnp.sum(sums[cg][k], axis=0, keepdims=True)

def mix_grad(l, act, gb):
    return lax.dot_general(act[l], gb[...], (((0,), (0,)), ((), ())), preferred_element_type=jnp.float32)


VM = pl.BlockSpec(memory_space=pltpu.VMEM)

class Reduction:
    def __init__(self, gm, final, out, c0, hh, r1, qq, r2, e8, r3, f8, ss, rs, ls):
        self.__dict__.update(gm=gm, final=final, out=out, ls=ls, c0=c0, hh=hh, r1=r1, qq=qq, r2=r2, e8=e8, r3=r3, f8=f8, ss=ss, rs=rs)
        self.h, self.w, self.x, self.z, self.c = h, w, x, z, c = coords()
        self.y = h * 2 + w
        others = lambda i, n: [lax.rem(i + k, n) for k in sorted(range(1, n), key=lambda k: -min(k, n - k))]
        self.on_axis = {1: [(j, place(h, w, j, z, c)) for j in others(x, 4)], 0: [(j, on_y(j, x, z, c)) for j in others(self.y, 4)]}
        self.on_z = [(j, place(h, w, x, j, c)) for j in others(z, 8)]

    def first(self, l):
        return self.x if l % 2 else self.y

    def second(self, l):
        return self.y if l % 2 else self.x

    def copy(self, src, dst, l, stage, dev):
        return pltpu.make_async_remote_copy(src, dst, self.ss.at[l, stage], self.rs.at[l, stage], device_id=dev, device_id_type=MESH)

    def other_core(self):
        return place(self.h, self.w, self.x, self.z, 1 - self.c)

    def rows(self, l):
        r256 = self.c * 256
        r64 = r256 + self.first(l) * 64
        return pl.multiple_of(r256, 256), pl.multiple_of(r64, 64), pl.multiple_of(r64 + self.second(l) * 16, 16)

    def took(self, ref, l, stage):
        pltpu.make_async_copy(ref, ref, self.rs.at[l, stage]).wait()

    def gave(self, ref, l, stage):
        pltpu.make_async_copy(ref, ref, self.ss.at[l, stage]).wait()

    def halve(self, l):
        far = pl.multiple_of((1 - self.c) * 256, 256)
        self.copy(self.gm.at[l, pl.ds(far, 256)], self.c0.at[l], l, 0, self.other_core()).start()

    def quarter(self, l):
        self.took(self.c0.at[l], l, 0)
        near = self.rows(l)[0]
        self.hh[l] = (self.gm[l, pl.ds(near, 256)].astype(jnp.float32) + self.c0[l].astype(jnp.float32)).astype(jnp.bfloat16)
        i = self.first(l)
        for j, dev in self.on_axis[l % 2]:
            self.copy(self.hh.at[l, pl.ds(pl.multiple_of(j * 64, 64), 64)], self.r1.at[l, i], l, 1, dev).start()

    def sixteenth(self, l):
        self.took(self.r1.at[l, pl.ds(0, 3)], l, 1)
        i = self.first(l)
        s = self.hh[l, pl.ds(pl.multiple_of(i * 64, 64), 64)].astype(jnp.float32)
        for k in range(1, 4):
            s += self.r1[l, lax.rem(i + k, 4)].astype(jnp.float32)
        self.qq[l] = s.astype(jnp.bfloat16)
        i2 = self.second(l)
        for j, dev in self.on_axis[1 - l % 2]:
            self.copy(self.qq.at[l, pl.ds(pl.multiple_of(j * 16, 16), 16)], self.r2.at[l, i2], l, 2, dev).start()

    def tile(self, p):
        z = self.z
        for l in (2 * p, 2 * p + 1):
            self.took(self.r2.at[l, pl.ds(0, 3)], l, 2)
            i2 = self.second(l)
            s = self.qq[l, pl.ds(pl.multiple_of(i2 * 16, 16), 16)].astype(jnp.float32)
            for k in range(1, 4):
                s += self.r2[l, lax.rem(i2 + k, 4)].astype(jnp.float32)
            for cg in range(4):
                self.e8[p, l % 2 * 4 + cg] = s[:, cg * 128:cg * 128 + 128].astype(jnp.bfloat16)
        for j, dev in self.on_z:
            self.copy(self.e8.at[p, j], self.r3.at[p, z], 2 * p, 3, dev).start()

    def untile(self, p):
        z = self.z
        self.took(self.r3.at[p, pl.ds(0, 7)], 2 * p, 3)
        s = self.e8[p, z].astype(jnp.float32)
        for k in range(1, 8):
            s += self.r3[p, lax.rem(z + k, 8)].astype(jnp.float32)
        self.f8[p, z] = s.astype(jnp.bfloat16)
        for j, dev in self.on_z:
            self.copy(self.f8.at[p, z], self.f8.at[p, z], 2 * p, 4, dev).start()

    def unsixteenth(self, p):
        self.took(self.f8.at[p, pl.ds(0, 7)], 2 * p, 4)
        for l in (2 * p, 2 * p + 1):
            r16 = self.rows(l)[2]
            for cg in range(4):
                self.out[l, pl.ds(r16, 16), cg * 128:cg * 128 + 128] = self.f8[p, l % 2 * 4 + cg]
            mine = self.out.at[l, pl.ds(r16, 16)]
            for j, dev in self.on_axis[1 - l % 2]:
                self.copy(mine, mine, l, 5, dev).start()

    def unquarter(self, p):
        for l in (2 * p, 2 * p + 1):
            self.took(self.out.at[l, pl.ds(0, 48)], l, 5)
            mine = self.out.at[l, pl.ds(self.rows(l)[1], 64)]
            for j, dev in self.on_axis[l % 2]:
                self.copy(mine, mine, l, 6, dev).start()

    def unhalve(self, p):
        for l in (2 * p, 2 * p + 1):
            self.took(self.out.at[l, pl.ds(0, 192)], l, 6)
            mine = self.out.at[l, pl.ds(self.rows(l)[0], 256)]
            there = self.final.at[l, pl.ds(self.rows(l)[0], 256)]
            self.copy(mine, there, l, 7, self.other_core()).start()
            pltpu.make_async_copy(mine, there, self.ls.at[l]).start()

    def settle(self, p):
        for l in (2 * p, 2 * p + 1):
            self.gave(self.c0.at[l], l, 0)
            self.gave(self.r1.at[l, pl.ds(0, 3)], l, 1)
            self.gave(self.r2.at[l, pl.ds(0, 3)], l, 2)
            self.gave(self.out.at[l, pl.ds(0, 48)], l, 5)
            self.gave(self.out.at[l, pl.ds(0, 192)], l, 6)
        self.gave(self.r3.at[p, pl.ds(0, 7)], 2 * p, 3)
        self.gave(self.f8.at[p, pl.ds(0, 7)], 2 * p, 4)

    def finish(self, p):
        for l in (2 * p, 2 * p + 1):
            half = self.final.at[l, pl.ds(0, 256)]
            pltpu.make_async_copy(half, half, self.ls.at[l]).wait()
            self.gave(self.out.at[l, pl.ds(0, 256)], l, 7)
            self.took(half, l, 7)

class TapSums:
    def __init__(self, bufs, ss, rs):
        self.pair, self.quarters, *self.slots, self.done = bufs
        self.ss, self.rs = ss, rs
        self.h, self.w, self.x, self.z, self.c = coords()
        self.y = self.h * 2 + self.w

    def others(self, stage):
        h, w, x, z, c = self.h, self.w, self.x, self.z, self.c
        if stage == 0:
            return [(1 - c, place(h, w, x, z, 1 - c))]
        if stage in (1, 4):
            return [(j, place(h, w, j, z, c)) for j in (lax.rem(x + k, 4) for k in range(1, 4))]
        if stage == 2:
            return [(j, on_y(j, x, z, c)) for j in (lax.rem(self.y + k, 4) for k in range(1, 4))]
        return [(j, place(h, w, x, j, c)) for j in (lax.rem(z + k, 8) for k in range(1, 8))]

    def buf(self, stage):
        return (self.pair, *self.slots, self.done)[stage]

    def push(self, stage, i, src):
        for j, dev in self.others(stage):
            pltpu.make_async_remote_copy(src(j), self.buf(stage).at[i], self.ss.at[stage], self.rs.at[stage], device_id=dev, device_id_type=MESH).start()

    def send(self, stage, value):
        i = (self.c, self.x, self.y, self.z, self.x)[stage]
        buf = self.buf(stage)
        if stage == 1:
            for q in range(4):
                self.quarters[q] = value[:, q * 128:q * 128 + 128]
            buf[i] = self.quarters[i]
            self.push(1, i, lambda j: self.quarters.at[j])
        else:
            buf[i] = value
            self.push(stage, i, lambda j: buf.at[i])

    def came(self, stage):
        buf = self.buf(stage)
        part = buf.at[pl.ds(0, buf.shape[0] - 1)]
        pltpu.make_async_copy(part, part, self.rs.at[stage]).wait()

    def total(self, stage):
        self.came(stage)
        buf = self.buf(stage)
        s = buf[0]
        for k in range(1, buf.shape[0]):
            s += buf[k]
        return s

    def result(self, out):
        self.came(4)
        for q in range(4):
            out[:, q * 128:q * 128 + 128] = self.done[q]

    def finish(self):
        for stage in range(5):
            buf = self.buf(stage)
            part = buf.at[pl.ds(0, buf.shape[0] - 1)]
            pltpu.make_async_copy(part, part, self.ss.at[stage]).wait()

def reduction_scratch():
    b = lambda *s: pltpu.VMEM(s, jnp.bfloat16)
    D = pltpu.SemaphoreType.DMA
    return [b(6, 512, 512), b(6, 512, 512), b(6, 256, 512), b(6, 256, 512), b(6, 4, 64, 512), b(6, 64, 512), b(6, 4, 16, 512), b(3, 8, 16, 128), b(3, 8, 16, 128), b(3, 8, 16, 128), D((6, 8)), D((6, 8)), D((6,))]

def tap_scratch():
    D = pltpu.SemaphoreType.DMA
    return [pltpu.VMEM((2, 16, 512), jnp.float32)] + [pltpu.VMEM((n, 16, 128), jnp.float32) for n in (4, 4, 4, 8, 4)] + [D((5,)), D((5,))]

def entry_scratch():
    return [pltpu.SemaphoreType.REGULAR] * 2


def kernel(x_hbm, c_hbm, taps_ref, mix_hbm, o_hbm, gt_out, gm_out, *scratch):
    scratch = list(scratch)
    def take(n):
        got = scratch[:n]
        del scratch[:n]
        return got
    x_ref, c_ref, mix_ref, in_sems = take(4)
    ox, sx, rx, oc, sc, rc, og, sg, rg, tok = take(10)
    pair_sems, sems, loc = take(3)
    xf, act, dg, g, gb, lag, gt = take(7)
    gm, *rest = take(13)
    red = Reduction(gm, gm_out, *rest)
    *bufs, tss, trs = take(8)
    taps = TapSums(bufs, tss, trs)
    plane_sem, all_sem = take(2)
    h, w, x, z, c = coords()

    greet()
    loads = [pltpu.make_async_copy(s, d, in_sems.at[i]) for i, (s, d) in enumerate(((x_hbm, x_ref), (c_hbm, c_ref), (mix_hbm, mix_ref)))]
    for load in loads:
        load.start()
    xf[:, :, 0:PAD] = jnp.zeros((LEVELS, 4, PAD, 128), jnp.float32)
    lag[:, 512:512 + PAD] = jnp.zeros((4, PAD, 128), jnp.float32)
    gt[...] = jnp.zeros((16, 512), jnp.float32)
    meet(plane_sem)
    loads[0].wait()
    tokens_to_tiles(x_ref, sx, ox, c)
    enter(plane_sem, all_sem)
    px = pair_copy(ox, sx, pair_sems, 0)
    px.start()
    spread_one(sx, rx, sems, loc, 0, c)
    loads[1].wait()
    tokens_to_tiles(c_ref, sc, oc, c)
    pc = pair_copy(oc, sc, pair_sems, 1)
    pc.start()
    px.wait_recv()
    spread_one(sx, rx, sems, loc, 3, 1 - c)
    one_arrived(sx, rx, sems, loc, 0)
    pc.wait_recv()
    spread(sc, rc, sems, loc, 1)
    loads[2].wait()
    one_arrived(sx, rx, sems, loc, 3)
    def put_x(i, cg, t):
        xf[0, cg, pl.ds(pl.multiple_of(PAD + i * 64, 32), 64)] = t
    tiles_to_rows(rx, put_x)
    for l in range(LEVELS):
        forward(l, xf, act, dg, taps_ref, mix_ref)

    spread_arrived(sc, rc, sems, loc, 1)
    def put_c(i, cg, t):
        rows = pl.ds(pl.multiple_of(i * 64, 64), 64)
        g[cg, rows] = t
        gb[rows, cg * 128:cg * 128 + 128] = t.astype(jnp.bfloat16)
    tiles_to_rows(rc, put_c)

    for l in reversed(range(LEVELS)):
        gm[l] = mix_grad(l, act, gb).astype(jnp.bfloat16)
        red.halve(l)
        backward(l, xf, dg, g, gb, lag, taps_ref, mix_ref, gt)
        if l == 3:
            red.quarter(5)
            red.quarter(4)
        if l == 2:
            red.quarter(3)
        if l == 1:
            red.quarter(2)

    red.sixteenth(5)
    red.sixteenth(4)
    red.sixteenth(3)
    red.quarter(1)
    red.quarter(0)
    red.sixteenth(2)
    rows_to_tiles(gb, sg, og, c)
    pg = pair_copy(og, sg, pair_sems, 2)
    pg.start()
    taps.send(0, gt[...])
    red.tile(2)
    red.tile(1)
    pg.wait_recv()
    spread(sg, rg, sems, loc, 2, 1, 8)
    spread(sg, rg, sems, loc, 2, 8, 16)
    red.sixteenth(0)
    taps.send(1, taps.total(0))
    red.sixteenth(1)
    red.untile(2)
    spread(sg, rg, sems, loc, 2, 16, 24)
    red.untile(1)
    red.tile(0)
    spread(sg, rg, sems, loc, 2, 24, 32)
    red.unsixteenth(2)
    spread(sg, rg, sems, loc, 2, 32, 40)
    spread(sg, rg, sems, loc, 2, 40, 48)
    red.unsixteenth(1)
    red.unquarter(2)
    red.untile(0)
    spread(sg, rg, sems, loc, 2, 48, 56)
    taps.send(2, taps.total(1))
    spread(sg, rg, sems, loc, 2, 56, 64)
    red.unsixteenth(0)
    red.unquarter(1)
    taps.send(3, taps.total(2))
    red.unhalve(2)
    red.unquarter(0)
    red.unhalve(1)
    spread_arrived(sg, rg, sems, loc, 2)
    tiles_to_tokens(rg, tok)
    tokens = pltpu.make_async_copy(tok, o_hbm, in_sems.at[0])
    tokens.start()
    taps.send(4, taps.total(3))
    red.unhalve(0)
    taps.result(gt_out)
    taps.finish()
    px.wait_send()
    pc.wait_send()
    pg.wait_send()
    one_sent(sx, rx, sems, 0)
    one_sent(sx, rx, sems, 3)
    spread_sent(sc, rc, sems, 1)
    spread_sent(sg, rg, sems, 2)
    for p in (2, 1, 0):
        red.settle(p)
    tokens.wait()
    for p in (2, 1, 0):
        red.finish(p)

def finish(o, gt, gm, o_out, gt_out, gm_out, held_o, held, sems, o_sems):
    ins = [pltpu.make_async_copy(gm.at[l], held.at[l], sems.at[0, l]) for l in range(LEVELS)]
    outs = [pltpu.make_async_copy(held.at[l], gm_out.at[l], sems.at[1, l]) for l in range(LEVELS)]
    for i in range(2):
        rows = pl.ds(i * 256, 256)
        ins.append(pltpu.make_async_copy(o.at[rows], held_o.at[rows], o_sems.at[0, i]))
        outs.append(pltpu.make_async_copy(held_o.at[rows], o_out.at[rows], o_sems.at[1, i]))
    for move in ins:
        move.start()
    for l in range(LEVELS):
        gt_out[l] = gt[2 * l:2 * l + 2]
    for i, move in enumerate(ins):
        move.wait()
        outs[i].start()
    for move in outs:
        move.wait()

def local(inputs, filter_taps, mixing, cotangent):
    f, b = jnp.float32, jnp.bfloat16
    V, S, D = pltpu.VMEM, jax.ShapeDtypeStruct, pltpu.SemaphoreType.DMA
    ANY = pl.BlockSpec(memory_space=pl.ANY)
    loaded = [V((512, 512), b), V((512, 512), b), V((LEVELS, 512, 512), b), D((3,))]
    exchange = ([V((64, 16, 128), b), V((64, 2, 16, 128), b), V((64, 2, 16, 128), b)] * 3) + [V((512, 512), f), D((2, 3)), D((2, 4)), D((4,))]
    levels = [V((LEVELS, 4, PAD + 512, 128), f), V((LEVELS, 512, 512), b), V((LEVELS, 4, 512, 128), f), V((4, 512, 128), f), V((512, 512), b), V((4, 512 + PAD, 128), f), V((16, 512), f)]
    o, gt, gm = pl.pallas_call(
        kernel,
        out_shape=[S((512, 512), f), S((16, 512), f), S((LEVELS, 512, 512), b)],
        in_specs=[ANY, ANY, VM, ANY],
        out_specs=[ANY, VM, ANY],
        scratch_shapes=loaded + exchange + levels + reduction_scratch() + tap_scratch() + entry_scratch(),
        compiler_params=pltpu.CompilerParams(collective_id=1, has_side_effects=True, vmem_limit_bytes=60 << 20),
        cost_estimate=pl.CostEstimate(flops=4831838208, bytes_accessed=10 << 20, transcendentals=1572864),
    )(inputs[0], cotangent[0], filter_taps, mixing)
    o, gt, gm = pl.pallas_call(
        finish,
        out_shape=[S((512, 512), f), S((LEVELS, 2, 512), f), S((LEVELS, 512, 512), b)],
        in_specs=[ANY, VM, ANY],
        out_specs=[ANY, VM, ANY],
        scratch_shapes=[V((512, 512), f), V((LEVELS, 512, 512), b), D((2, LEVELS)), D((2, 2))],
        compiler_params=pltpu.CompilerParams(vmem_limit_bytes=60 << 20),
    )(o, gt, gm)
    return o[None], gt, gm

def solution(mesh):
    halves = P("dp", "seq", None)
    return jax.shard_map(local, mesh=mesh, in_specs=(halves, P(), P(), halves), out_specs=(halves, P(), P()), check_vma=False)
```
